256 devices in a mesh: cuts: 16 (over x_hi, y, core), row: 16 (over z, x_lo).
Axes of the slice: x: 4 (x_hi: 2, x_lo: 2; x = x_hi * 2 + x_lo), y: 4, z: 8, core: 2. Of those that a mesh axis runs over, the one named last changes fastest.
Arguments:
- vectors: float32 [16, 65536, 192], P('cuts', 'row'), as said below
- images: float32 [16, 65536, 192], P('cuts', 'row'), as said below
- kept_flags: int32 [16, 192], replicated, may hold values from 0 to 1, as said below
Outputs:
- residual: float32 [16, 65536, 192], P('cuts', 'row')
- kept_columns: float32 [16, 65536, 96], P('cuts', 'row')
The draws below stay inside these ranges and needn't reach their ends.
Inputs may be any that keep to these rules, and one draw needn't show every extreme that they name: `vectors`: no structure is promised. `images`: no structure is promised. `kept_flags`: slices 0 to s together keep between 96 * (s + 1) and 96 * (s + 2) - 1 columns, and all slices together exactly 1536; in every draw, for some s below the last slice, slices 0 to s keep exactly 96 * (s + 2) - 1.
All inputs are finite; a program needn't handle non-finite values.
Results may differ from the reference program's by a relative error of at most 0.0003.
Values sent between devices are 32-bit elements; how exact they have to be, the bound alone decides.
A program may use at most 64 MiB of HBM per device.

```python
import math
import jax
import jax.numpy as jnp
from jax import lax

W = 192
SHARED = 64
KEEP_DEV = 96
SLICES = 16
NROWS = 65536


def shared_basis(key):
    keys = jax.random.split(key, 5)
    raw = jax.random.normal(keys[0], (SLICES, NROWS, W), jnp.float32)
    mixed = raw + 0.5 * jnp.roll(raw, 1, axis=2)
    tail_prev = jnp.roll(mixed[:, :, W - SHARED:], 1, axis=0)
    slice_ids = jnp.arange(SLICES)[:, None, None]
    head = jnp.where(slice_ids > 0, 0.6 * mixed[:, :, :SHARED] + 0.8 * tail_prev, mixed[:, :, :SHARED])
    mixed = jnp.concatenate([head, mixed[:, :, SHARED:]], 2)
    scales = 0.5 * jnp.exp(jax.random.uniform(keys[2], (SLICES, 1, W), jnp.float32) * math.log(10.0))
    basis = mixed * scales
    levels = jax.random.uniform(keys[3], (SLICES, 1, W), jnp.float32, -2.0, 2.0)
    noise = 0.3 * scales * jax.random.normal(keys[4], (SLICES, NROWS, W), jnp.float32)
    return (basis, levels * basis + noise)


def draw_vectors(key, part):
    basis, applied = shared_basis(key)
    return basis


def draw_images(key, part):
    basis, applied = shared_basis(key)
    return applied


def draw_kept_flags(key, part):
    key = jax.random.fold_in(key, 11)
    keys = jax.random.split(key, 3)
    slice_ids = jnp.arange(SLICES, dtype=jnp.int32)
    drift = jax.random.randint(keys[0], (SLICES,), 0, KEEP_DEV, jnp.int32)
    chosen = jax.random.randint(keys[1], (), 0, SLICES - 1, jnp.int32)
    drift = jnp.where(slice_ids == chosen, KEEP_DEV - 1, drift)
    drift = jnp.where(slice_ids == SLICES - 1, 0, drift)
    before = jnp.concatenate([jnp.zeros((1,), jnp.int32), drift[:-1]])
    counts = KEEP_DEV + drift - before
    scores = jax.random.randint(keys[2], (SLICES, W), 0, 1 << 20, jnp.int32) * W + jnp.arange(W, dtype=jnp.int32)[None, :]
    ranks = jnp.argsort(jnp.argsort(scores, axis=1), axis=1)
    return (ranks < counts[:, None]).astype(jnp.int32)


def setup_inputs(seed: int = 0) -> dict:
    streams_of = jax.random.split(jax.random.key(seed), 4)
    vectors = draw_vectors(jax.random.fold_in(streams_of[3], 71), 0)
    images = draw_images(jax.random.fold_in(streams_of[3], 71), 0)
    kept_flags = draw_kept_flags(jax.random.fold_in(streams_of[3], 71), 0)
    return {"vectors": vectors, "images": images, "kept_flags": kept_flags}


def blend_one(own, below, above, slice_id):
    width = own.shape[1]
    head = jnp.where(slice_id > 0, 0.5 * (own[:, :SHARED] + below[:, width - SHARED:]), own[:, :SHARED])
    tail = jnp.where(slice_id < SLICES - 1, 0.5 * (own[:, width - SHARED:] + above[:, :SHARED]), own[:, width - SHARED:])
    return jnp.concatenate([head, own[:, SHARED:width - SHARED], tail], 1)

def solve_coeff(gram, projected):
    factor = jnp.linalg.cholesky(gram)
    middle = jax.scipy.linalg.solve_triangular(factor, projected, lower=True)
    return jax.scipy.linalg.solve_triangular(factor, middle, lower=True, trans=1)

def reference(vectors, images, kept_flags):
    high = lax.Precision.HIGHEST

    def one_slice(slice_id):
        lower = jnp.maximum(slice_id - 1, 0)
        upper = jnp.minimum(slice_id + 1, SLICES - 1)
        basis = blend_one(vectors[slice_id], vectors[lower], vectors[upper], slice_id)
        applied = blend_one(images[slice_id], images[lower], images[upper], slice_id)
        gram = lax.dot_general(basis.astype(jnp.float32), basis.astype(jnp.float32), (((0,), (0,)), ((), ())), precision=high, preferred_element_type=jnp.float32)
        projected = lax.dot_general(basis.astype(jnp.float32), applied.astype(jnp.float32), (((0,), (0,)), ((), ())), precision=high, preferred_element_type=jnp.float32)
        coeff = solve_coeff(gram, projected)
        rotated = jnp.dot(basis.astype(jnp.float32), coeff.astype(jnp.float32), precision=high, preferred_element_type=jnp.float32)
        return (applied - rotated, rotated)
    residual, rotated = lax.map(one_slice, jnp.arange(SLICES, dtype=jnp.int32))
    width = vectors.shape[2]
    flat = kept_flags.reshape(-1)
    order = jnp.argsort(1 - flat, stable=True)[:SLICES * KEEP_DEV].astype(jnp.int32)
    source = order // width
    column = order % width
    picked = rotated[source, :, column]
    kept_columns = picked.reshape(SLICES, KEEP_DEV, NROWS).transpose(0, 2, 1)
    return (residual, kept_columns)
```

```python
import functools

import jax
import jax.numpy as jnp
from jax import lax
from jax.experimental import pallas as pl
from jax.experimental.pallas import tpu as pltpu
from jax.sharding import PartitionSpec as P

W = 192
SHARED = 64
KEEP_DEV = 96
SLICES = 16
ROWS = 4096
PEERS = 16
CHUNKS = 4
CHUNK = ROWS // CHUNKS
LANES = 256
PACK_G = 256
PACK_P = 384
F32 = jnp.float32
HIGH = lax.Precision.HIGHEST
MESH = pl.DeviceIdType.MESH
ANY = pl.BlockSpec(memory_space=pl.ANY)
VMEM = pl.BlockSpec(memory_space=pltpu.VMEM)


def dot_rows(a, b):
    return lax.dot_general(a, b, (((1,), (1,)), ((), ())), precision=HIGH, preferred_element_type=F32)


def dot(a, b):
    return lax.dot_general(a, b, (((1,), (0,)), ((), ())), precision=HIGH, preferred_element_type=F32)


def sweep_block(kb, a_ref, d_ref):
    base = pl.multiple_of(kb * 8, 8)
    lane = lax.broadcasted_iota(jnp.int32, (8, LANES), 1) - base
    in_block = jnp.logical_and(lane >= 0, lane < 8)
    diag = a_ref[pl.ds(base, 8), pl.ds(pl.multiple_of((kb // 16) * 128, 128), 128)]
    diag = pltpu.roll(diag, lax.rem(128 - lax.rem(base, 128), 128), 1)
    for j in range(8):
        d_ref[j] = jnp.broadcast_to(diag[:, j : j + 1], (8, 128))
    d = {}
    for i in range(8):
        for j in range(i, 8):
            d[i, j] = jnp.broadcast_to(d_ref[j, i : i + 1, :], (8, 128))

    def at(i, j):
        return d[min(i, j), max(i, j)]

    for k in range(8):
        pivot = 1.0 / d[k, k]
        scaled = {i: at(i, k) * pivot for i in range(8) if i != k}
        for i in range(8):
            for j in range(i, 8):
                if i != k and j != k:
                    d[i, j] = d[i, j] - scaled[i] * at(j, k)
        for i in range(8):
            if i != k:
                d[min(i, k), max(i, k)] = scaled[i]
        d[k, k] = -pivot
    rows = []
    for j in range(8):
        row = jnp.broadcast_to(a_ref[pl.ds(base + j, 1), :], (8, LANES))
        rows.append(jnp.where(in_block, jnp.where(lane == j, 1.0, 0.0), -row))
    solved = []
    for i in range(8):
        total = None
        for j in range(8):
            term = jnp.concatenate([at(i, j)] * 2, 1) * rows[j]
            total = term if total is None else total + term
        solved.append(total)
    columns = a_ref[pl.ds(base, 8), :].T
    for t in range(W // 8):
        total = jnp.where(in_block, 0.0, a_ref[8 * t : 8 * t + 8, :])
        for j in range(8):
            total = total - jnp.broadcast_to(columns[8 * t : 8 * t + 8, j : j + 1], (8, LANES)) * solved[j]
        a_ref[8 * t : 8 * t + 8, :] = total
    sublane = lax.broadcasted_iota(jnp.int32, (8, LANES), 0)
    mine = solved[0]
    for i in range(1, 8):
        mine = jnp.where(sublane == i, solved[i], mine)
    a_ref[pl.ds(base, 8), :] = mine


def solve_kernel(
    v_hbm, i_hbm, flags_ref,
    x_out, y_out, xp_out, c_ref, kp_ref,
    x, y, tv, hv, ti, hi, gram, proj, gpack, gparts, gfull, ppack, pparts, pfull, mine_g, mine_p,
    a_ref, d_ref, kn, kp,
    load_sem, ex_send, ex_recv, sum_send, sum_recv, fwd_send, fwd_recv, out_sem,
):
    s = lax.axis_index("cuts")
    r = lax.axis_index("row")
    has_lower = s > 0
    has_upper = s < SLICES - 1
    upper = lax.rem(s + 1, SLICES)
    lower = lax.rem(s + SLICES - 1, SLICES)

    load_x = pltpu.make_async_copy(v_hbm, x, load_sem.at[0])
    load_y = pltpu.make_async_copy(i_hbm, y, load_sem.at[1])
    load_x.start()
    load_y.start()

    barrier = pltpu.get_barrier_semaphore()
    for q in (lower, upper):
        pl.semaphore_signal(barrier, inc=1, device_id=(q, r), device_id_type=MESH)

    def greet(i, carry):
        pl.semaphore_signal(barrier, inc=1, device_id=(s, lax.rem(r + i, PEERS)), device_id_type=MESH)
        return carry

    lax.fori_loop(1, PEERS, greet, 0)
    pl.semaphore_wait(barrier, PEERS + 1)

    def lanes(c):
        return pl.ds(pl.multiple_of(c * CHUNK, CHUNK), CHUNK)

    def exchange(kind, c, up):
        src = (v_hbm, i_hbm)[kind]
        dst = ((tv, ti), (hv, hi))[0 if up else 1][kind]
        first = W - SHARED if up else 0
        way = 0 if up else 1
        return pltpu.make_async_remote_copy(
            src_ref=src.at[pl.ds(first, SHARED), lanes(c)],
            dst_ref=dst.at[:, lanes(c)],
            send_sem=ex_send.at[kind, way, c],
            recv_sem=ex_recv.at[kind, way, c],
            device_id=(upper if up else lower, r),
            device_id_type=MESH,
        )

    def send(kind, c):
        @pl.when(has_upper)
        def _():
            exchange(kind, c, True).start()

        @pl.when(has_lower)
        def _():
            exchange(kind, c, False).start()

    def receive(kind, c):
        @pl.when(has_lower)
        def _():
            exchange(kind, c, True).wait_recv()

        @pl.when(has_upper)
        def _():
            exchange(kind, c, False).wait_recv()

    def blend(own, low, high, c):
        head = own[0:SHARED, lanes(c)]
        tail = own[W - SHARED : W, lanes(c)]
        own[0:SHARED, lanes(c)] = jnp.where(has_lower, 0.5 * (head + low[:, lanes(c)]), head)
        own[W - SHARED : W, lanes(c)] = jnp.where(has_upper, 0.5 * (tail + high[:, lanes(c)]), tail)

    for c in range(CHUNKS):
        send(0, c)
    load_x.wait()
    gram[...] = jnp.zeros_like(gram)
    proj[...] = jnp.zeros_like(proj)

    def gram_step(c, carry):
        receive(0, c)
        blend(x, tv, hv, c)
        part = x[:, lanes(c)]
        gram[...] += dot_rows(part, part)

        @pl.when(c == CHUNKS - 2)
        def _():
            send(1, 0)

        return carry

    lax.fori_loop(0, CHUNKS, gram_step, 0)
    for c in range(1, CHUNKS):
        send(1, c)

    def scatter(which, pack, parts, chunk):
        def one(i, carry):
            q = lax.rem(r + i, PEERS)
            pltpu.make_async_remote_copy(
                src_ref=pack.at[pl.ds(pl.multiple_of(q * chunk, 8), chunk), :],
                dst_ref=parts.at[i - 1],
                send_sem=sum_send.at[which],
                recv_sem=sum_recv.at[which],
                device_id=(s, q),
                device_id_type=MESH,
            ).start()
            return carry

        lax.fori_loop(1, PEERS, one, 0)

    def all_parts(which, parts):
        return pltpu.make_async_remote_copy(
            src_ref=parts,
            dst_ref=parts,
            send_sem=sum_send.at[which],
            recv_sem=sum_recv.at[which],
            device_id=(s, lax.rem(r + 1, PEERS)),
            device_id_type=MESH,
        )

    def add_parts(pack, parts, mine, full, chunk):
        place = pl.ds(pl.multiple_of(r * chunk, 8), chunk)
        total = pack[place, :]
        for i in range(PEERS - 1):
            total = total + parts[i]
        mine[...] = total
        full[place, :] = total

    def gather(which, mine, full, chunk):
        place = pl.ds(pl.multiple_of(r * chunk, 8), chunk)

        def one(i, carry):
            pltpu.make_async_remote_copy(
                src_ref=mine,
                dst_ref=full.at[place, :],
                send_sem=sum_send.at[which],
                recv_sem=sum_recv.at[which],
                device_id=(s, lax.rem(r + i, PEERS)),
                device_id_type=MESH,
            ).start()
            return carry

        lax.fori_loop(1, PEERS, one, 0)

    gpack[0:W, :] = gram[:, 0:128]
    gpack[W:PACK_G, 0:64] = gram[128:W, 128:W]
    gpack[W:PACK_G, 64:128] = jnp.zeros((64, 64), F32)
    scatter(0, gpack, gparts, PACK_G // PEERS)

    load_y.wait()

    def proj_step(c, carry):
        receive(1, c)
        blend(y, ti, hi, c)
        proj[...] += dot_rows(y[:, lanes(c)], x[:, lanes(c)])
        return carry

    lax.fori_loop(0, 1, proj_step, 0)

    all_parts(0, gparts).wait_recv()
    add_parts(gpack, gparts, mine_g, gfull, PACK_G // PEERS)
    gather(1, mine_g, gfull, PACK_G // PEERS)

    lax.fori_loop(1, CHUNKS, proj_step, 0)

    def forward(k):
        src = x.at[0:SHARED, :] if k == 0 else v_hbm.at[SHARED : 2 * SHARED, :]
        return pltpu.make_async_remote_copy(
            src_ref=src,
            dst_ref=xp_out.at[pl.ds(k * SHARED, SHARED), :],
            send_sem=fwd_send.at[k],
            recv_sem=fwd_recv.at[k],
            device_id=(upper, r),
            device_id_type=MESH,
        )

    save_x = pltpu.make_async_copy(x, x_out, out_sem.at[0])
    save_y = pltpu.make_async_copy(y, y_out, out_sem.at[1])
    fill = pltpu.make_async_copy(x.at[0:128, :], xp_out, out_sem.at[2])

    @pl.when(has_upper)
    def _():
        forward(1).start()
        forward(0).start()

    save_x.start()
    save_y.start()

    @pl.when(jnp.logical_not(has_lower))
    def _():
        fill.start()

    ppack[0:W, :] = proj[:, 0:128]
    ppack[W : 2 * W, 0:64] = proj[:, 128:W]
    ppack[W : 2 * W, 64:128] = jnp.zeros((W, 64), F32)
    scatter(2, ppack, pparts, PACK_P // PEERS)

    all_parts(1, gparts).wait_recv()
    a_ref[:, 0:128] = gfull[0:W, :]
    corner = jnp.concatenate([gfull[128:W, :].T, gfull[W:PACK_G, 0:64]], 0)
    a_ref[:, 128:LANES] = jnp.concatenate([corner, jnp.zeros((W, 64), F32)], 1)

    def sweep_step(kb, carry):
        sweep_block(kb, a_ref, d_ref)
        return carry

    lax.fori_loop(0, 12, sweep_step, 0)
    all_parts(2, pparts).wait_recv()
    add_parts(ppack, pparts, mine_p, pfull, PACK_P // PEERS)
    gather(3, mine_p, pfull, PACK_P // PEERS)
    lax.fori_loop(12, 24, sweep_step, 0)

    flags = flags_ref[...].astype(F32)
    row_id = lax.broadcasted_iota(jnp.int32, (SLICES, W), 0)
    before = jnp.sum(jnp.where(row_id < s, flags, 0.0), keepdims=True)
    own_flags = jnp.sum(jnp.where(row_id == s, flags, 0.0), axis=0, keepdims=True)
    earlier = lax.broadcasted_iota(jnp.int32, (W, W), 0) < lax.broadcasted_iota(jnp.int32, (W, W), 1)
    ranks = dot(jnp.broadcast_to(own_flags, (8, W)), jnp.where(earlier, 1.0, 0.0))[0:1]
    slot = ranks + before - (s * KEEP_DEV).astype(F32)
    slot_id = lax.broadcasted_iota(jnp.int32, (W, W), 0).astype(F32)
    select = jnp.where(jnp.logical_and(slot_id == slot, own_flags > 0.5), 1.0, 0.0)

    all_parts(3, pparts).wait_recv()
    proj_sum = jnp.concatenate([pfull[0:W, :], pfull[W : 2 * W, 0:64]], 1)
    coeff = dot(proj_sum, -a_ref[:, 0:W])
    placed = dot(select, coeff)
    kn[...] = placed[KEEP_DEV:W]

    late = pltpu.make_async_remote_copy(
        src_ref=kn,
        dst_ref=kp,
        send_sem=fwd_send.at[2],
        recv_sem=fwd_recv.at[2],
        device_id=(upper, r),
        device_id_type=MESH,
    )

    @pl.when(has_upper)
    def _():
        late.start()

    c_ref[0:W, :] = coeff

    for kind in range(2):
        for c in range(CHUNKS):

            @pl.when(has_upper)
            def _():
                exchange(kind, c, True).wait_send()

            @pl.when(has_lower)
            def _():
                exchange(kind, c, False).wait_send()

    all_parts(0, gparts).wait_send()
    all_parts(1, gparts).wait_send()
    all_parts(2, pparts).wait_send()
    all_parts(3, pparts).wait_send()
    save_x.wait()
    save_y.wait()

    @pl.when(jnp.logical_not(has_lower))
    def _():
        fill.wait()
        kp[...] = jnp.zeros_like(kp)

    @pl.when(has_lower)
    def _():
        forward(1).wait_recv()
        forward(0).wait_recv()
        late.wait_recv()

    previous = kp[...]
    shift = jnp.concatenate([previous[:, 128:W], jnp.zeros((KEEP_DEV, 128), F32)], 1)
    c_ref[W : W + KEEP_DEV, :] = placed[0:KEEP_DEV] + shift
    kp_ref[...] = previous[:, 0:128]

    @pl.when(has_upper)
    def _():
        forward(1).wait_send()
        forward(0).wait_send()
        late.wait_send()


def solve_call(vectors, images, flags):
    shape = jax.ShapeDtypeStruct
    big = pltpu.VMEM((W, ROWS), F32)
    shared = pltpu.VMEM((SHARED, ROWS), F32)
    dma = pltpu.SemaphoreType.DMA
    chunk_g, chunk_p = PACK_G // PEERS, PACK_P // PEERS
    return pl.pallas_call(
        solve_kernel,
        out_shape=(
            shape((W, ROWS), F32), shape((W, ROWS), F32), shape((2 * SHARED, ROWS), F32),
            shape((W + KEEP_DEV, W), F32), shape((KEEP_DEV, 2 * SHARED), F32),
        ),
        in_specs=[ANY, ANY, VMEM],
        out_specs=(ANY, ANY, ANY, VMEM, VMEM),
        scratch_shapes=[
            big, big, shared, shared, shared, shared,
            pltpu.VMEM((W, W), F32), pltpu.VMEM((W, W), F32),
            pltpu.VMEM((PACK_G, 128), F32), pltpu.VMEM((PEERS - 1, chunk_g, 128), F32), pltpu.VMEM((PACK_G, 128), F32),
            pltpu.VMEM((PACK_P, 128), F32), pltpu.VMEM((PEERS - 1, chunk_p, 128), F32), pltpu.VMEM((PACK_P, 128), F32),
            pltpu.VMEM((chunk_g, 128), F32), pltpu.VMEM((chunk_p, 128), F32),
            pltpu.VMEM((W, LANES), F32), pltpu.VMEM((8, 8, 128), F32),
            pltpu.VMEM((KEEP_DEV, W), F32), pltpu.VMEM((KEEP_DEV, W), F32),
            dma((2,)), dma((2, 2, CHUNKS)), dma((2, 2, CHUNKS)), dma((4,)), dma((4,)), dma((3,)), dma((3,)), dma((3,)),
        ],
        compiler_params=pltpu.CompilerParams(
            collective_id=0, has_side_effects=True, vmem_limit_bytes=40 << 20
        ),
        name="exchange_and_solve",
    )(vectors, images, flags)


def rotate_kernel(x_ref, y_ref, xp_ref, c_ref, kp_ref, res_ref, kept_ref):
    both = dot(c_ref[...], x_ref[...])
    res_ref[...] = y_ref[...] - both[0:W]
    kept_ref[...] = both[W : W + KEEP_DEV] + dot(kp_ref[...], xp_ref[...])


def rotate_call(x, y, xp, c, kp):
    block = 512

    def tall(rows):
        return pl.BlockSpec((rows, block), lambda i: (0, i))

    def whole(shape):
        return pl.BlockSpec(shape, lambda i: (0, 0))

    return pl.pallas_call(
        rotate_kernel,
        grid=(ROWS // block,),
        out_shape=(jax.ShapeDtypeStruct((W, ROWS), F32), jax.ShapeDtypeStruct((KEEP_DEV, ROWS), F32)),
        in_specs=[tall(W), tall(W), tall(2 * SHARED), whole((W + KEEP_DEV, W)), whole((KEEP_DEV, 2 * SHARED))],
        out_specs=(tall(W), tall(KEEP_DEV)),
        compiler_params=pltpu.CompilerParams(vmem_limit_bytes=40 << 20),
        name="rotate",
    )(x, y, xp, c, kp)


def on_device(vectors, images, kept_flags):
    x, y, xp, c, kp = solve_call(vectors[0].T, images[0].T, kept_flags)
    residual, kept = rotate_call(x, y, xp, c, kp)
    return residual.T[None], kept.T[None]


def solution(mesh):
    placed = (P("cuts", "row", None), P("cuts", "row", None), P())
    return jax.shard_map(
        on_device,
        mesh=mesh,
        in_specs=placed,
        out_specs=(P("cuts", "row", None), P("cuts", "row", None)),
        check_vma=False,
    )
```

```python
import functools

import jax
import jax.numpy as jnp
from jax import lax
from jax.experimental import pallas as pl
from jax.experimental.pallas import tpu as pltpu
from jax.sharding import PartitionSpec as P

W = 192
SHARED = 64
KEEP_DEV = 96
SLICES = 16
ROWS = 4096
PEERS = 16
CHUNKS = 4
CHUNK = ROWS // CHUNKS
EARLY = 2
EARLY_ROWS = EARLY * CHUNK
LANES = 256
PANEL = 48
VMEM_LIMIT = 48 << 20
PACK = (256, 256, 128)
F32 = jnp.float32
BF16 = jnp.bfloat16
HIGH = lax.Precision.HIGHEST
MESH = pl.DeviceIdType.MESH
HBM = pl.BlockSpec(memory_space=pltpu.HBM)
VMEM = pl.BlockSpec(memory_space=pltpu.VMEM)


def split(a):
    high = a.astype(BF16)
    return high, (a - high.astype(F32)).astype(BF16)


def dot_rows(a, b):
    return lax.dot_general(a, b, (((1,), (1,)), ((), ())), preferred_element_type=F32)


def dot_split(a, b):
    def one(x, y):
        return lax.dot_general(x, y, (((1,), (0,)), ((), ())), preferred_element_type=F32)

    return one(a[0], b[0]) + (one(a[0], b[1]) + one(a[1], b[0]))


def dot(a, b):
    return lax.dot_general(a, b, (((1,), (0,)), ((), ())), precision=HIGH, preferred_element_type=F32)


def sweep_block(kb, q, p_ref, d_ref):
    base = kb * 8
    first = 8 * q
    lane = lax.broadcasted_iota(jnp.int32, (8, LANES), 1) - base
    in_block = jnp.logical_and(lane >= 0, lane < 8)
    half = pl.ds(pl.multiple_of((kb // 16) * 128, 128), 128)
    turn = lax.rem(128 - lax.rem(base, 128), 128)
    pivots = {z: pltpu.roll(p_ref[8 * z : 8 * z + 8, half], turn, 1) for z in range(PANEL // 8)}
    for j in range(8):
        d_ref[j] = jnp.broadcast_to(pivots[q][:, j : j + 1], (8, 128))
    d = {}
    for i in range(8):
        for j in range(i, 8):
            d[i, j] = jnp.broadcast_to(d_ref[j, i : i + 1, :], (8, 128))

    def at(i, j):
        return d[min(i, j), max(i, j)]

    for k in range(8):
        pivot = 1.0 / d[k, k]
        scaled = {i: at(i, k) * pivot for i in range(8) if i != k}
        for i in range(8):
            for j in range(i, 8):
                if i != k and j != k:
                    d[i, j] = d[i, j] - scaled[i] * at(j, k)
        for i in range(8):
            if i != k:
                d[min(i, k), max(i, k)] = scaled[i]
        d[k, k] = -pivot
    rows = []
    for j in range(8):
        row = jnp.broadcast_to(p_ref[first + j : first + j + 1, :], (8, LANES))
        rows.append(jnp.where(in_block, jnp.where(lane == j, 1.0, 0.0), -row))
    solved = []
    for i in range(8):
        total = None
        for j in range(8):
            term = jnp.concatenate([at(i, j)] * 2, 1) * rows[j]
            total = term if total is None else total + term
        solved.append(total)
    for z in range(PANEL // 8):
        if z != q:
            total = jnp.where(in_block, 0.0, p_ref[8 * z : 8 * z + 8, :])
            for j in range(8):
                total = total - jnp.broadcast_to(pivots[z][:, j : j + 1], (8, LANES)) * solved[j]
            p_ref[8 * z : 8 * z + 8, :] = total
    sublane = lax.broadcasted_iota(jnp.int32, (8, LANES), 0)
    mine = solved[0]
    for i in range(1, 8):
        mine = jnp.where(sublane == i, solved[i], mine)
    p_ref[first : first + 8, :] = mine


def sweep_panel(step, a_ref, p_ref, d_ref):
    base = pl.multiple_of(step * PANEL, PANEL)
    panel = a_ref[pl.ds(base, PANEL), :]
    p_ref[...] = panel
    for q in range(PANEL // 8):
        sweep_block(step * (PANEL // 8) + q, q, p_ref, d_ref)
    swept = p_ref[...]
    update = lax.dot_general(
        panel[:, 0:W], swept, (((0,), (0,)), ((), ())), precision=HIGH, preferred_element_type=F32
    )
    lane = lax.broadcasted_iota(jnp.int32, (W, LANES), 1) - base
    a_ref[...] = jnp.where(jnp.logical_and(lane >= 0, lane < PANEL), 0.0, a_ref[...]) - update
    a_ref[pl.ds(base, PANEL), :] = swept


def fused_kernel(
    v_hbm, i_hbm, flags_ref,
    res_ref, kept_ref,
    x, y, xh, xl, fv, fi, sv, si, xp, z_out, z_in, g_hh, g_hl, proj,
    pack_g, pack_f, pack_s, parts_g, parts_f, parts_s, mine_g, mine_f, mine_s, full_g, full_f, full_s,
    a_ref, p_ref, d_ref, pt_ref, select, kn, kp, lhs_h, lhs_l,
    load_sem, ex_send, ex_recv, sum_send, sum_recv, fwd_send, fwd_recv,
):
    s = lax.axis_index("cuts")
    r = lax.axis_index("row")
    odd = lax.rem(s, 2)
    has_lower = s > 0
    has_upper = s < SLICES - 1
    has_slow = jnp.logical_and(has_lower, has_upper)
    paced = jnp.logical_or(s == SLICES // 2 - 1, s == SLICES // 2)
    unpaced = jnp.logical_and(has_slow, jnp.logical_not(paced))
    upper = lax.rem(s + 1, SLICES)
    near = s + 1 - 2 * odd
    far = lax.rem(s + SLICES - 1 + 2 * odd, SLICES)
    near_row = pl.multiple_of(128 - 128 * odd, 64)
    far_row = pl.multiple_of(128 * odd, 64)
    rest_row = pl.multiple_of(64 - 64 * odd, 64)

    load_x = pltpu.make_async_copy(v_hbm, x, load_sem.at[0])
    load_y = pltpu.make_async_copy(i_hbm, y, load_sem.at[1])
    load_x.start()
    load_y.start()

    barrier = pltpu.get_barrier_semaphore()
    for q in (near, far):
        pl.semaphore_signal(barrier, inc=1, device_id=(q, r), device_id_type=MESH)

    def greet(i, carry):
        pl.semaphore_signal(barrier, inc=1, device_id=(s, lax.rem(r + i, PEERS)), device_id_type=MESH)
        return carry

    lax.fori_loop(1, PEERS, greet, 0)

    flags = flags_ref[...].astype(F32)
    row_id = lax.broadcasted_iota(jnp.int32, (SLICES, W), 0)
    before = jnp.sum(jnp.where(row_id < s, flags, 0.0), keepdims=True)
    own_flags = jnp.sum(jnp.where(row_id == s, flags, 0.0), axis=0, keepdims=True)
    earlier = lax.broadcasted_iota(jnp.int32, (W, W), 0) < lax.broadcasted_iota(jnp.int32, (W, W), 1)
    ranks = dot(jnp.broadcast_to(own_flags, (8, W)), jnp.where(earlier, 1.0, 0.0))[0:1]
    slot = ranks + before - (s * KEEP_DEV).astype(F32)
    slot_id = lax.broadcasted_iota(jnp.int32, (W, W), 0).astype(F32)
    select[...] = jnp.where(jnp.logical_and(slot_id == slot, own_flags > 0.5), 1.0, 0.0)
    for ref in (g_hh, g_hl, proj, pack_g, pack_f, pack_s):
        ref[...] = jnp.zeros_like(ref)

    pl.semaphore_wait(barrier, PEERS + 1)

    def lanes(c):
        return pl.ds(pl.multiple_of(c * CHUNK, CHUNK), CHUNK)

    def exchange(kind, c, way):
        return pltpu.make_async_remote_copy(
            src_ref=(v_hbm, i_hbm)[kind].at[pl.ds((near_row, far_row)[way], SHARED), lanes(c)],
            dst_ref=((fv, sv), (fi, si))[kind][way].at[:, lanes(c)],
            send_sem=ex_send.at[kind, way, c],
            recv_sem=ex_recv.at[kind, way, c],
            device_id=((near, far)[way], r),
            device_id_type=MESH,
        )

    def when_slow(action):
        pl.when(has_slow)(action)

    def blend(own, other, row, c):
        mine = own[pl.ds(row, SHARED), lanes(c)]
        own[pl.ds(row, SHARED), lanes(c)] = 0.5 * (mine + other[:, lanes(c)])

    for c in range(CHUNKS):
        when_slow(lambda c=c: exchange(0, c, 1).start())
        exchange(0, c, 0).start()
    for c in range(CHUNKS):
        exchange(1, c, 0).start()
    load_x.wait()

    def gram_step(c, carry):
        exchange(0, c, 0).wait_recv()
        blend(x, fv, near_row, c)

        @pl.when(has_slow)
        def _():
            exchange(0, c, 1).wait_recv()
            blend(x, sv, far_row, c)

        high, low = split(x[:, lanes(c)])
        xh[:, lanes(c)] = high
        xl[:, lanes(c)] = low
        g_hh[...] += dot_rows(high, high)
        g_hl[...] += dot_rows(high, low)

        @pl.when(jnp.logical_and(unpaced, c == CHUNKS - 2))
        def _():
            exchange(1, 0, 1).start()

        return carry

    lax.fori_loop(0, CHUNKS, gram_step, 0)
    for c in range(1, CHUNKS):
        pl.when(unpaced)(lambda c=c: exchange(1, c, 1).start())

    sums = (
        (pack_g, parts_g, mine_g, full_g, PACK[0] // PEERS),
        (pack_f, parts_f, mine_f, full_f, PACK[1] // PEERS),
        (pack_s, parts_s, mine_s, full_s, PACK[2] // PEERS),
    )

    def scatter(which):
        pack, parts, _, _, chunk = sums[which]

        def one(i, carry):
            q = lax.rem(r + i, PEERS)
            pltpu.make_async_remote_copy(
                src_ref=pack.at[pl.ds(pl.multiple_of(q * chunk, 8), chunk), :],
                dst_ref=parts.at[i - 1],
                send_sem=sum_send.at[0, which],
                recv_sem=sum_recv.at[0, which],
                device_id=(s, q),
                device_id_type=MESH,
            ).start()
            return carry

        lax.fori_loop(1, PEERS, one, 0)

    def arrived(phase, which):
        parts = sums[which][1]
        return pltpu.make_async_remote_copy(
            src_ref=parts,
            dst_ref=parts,
            send_sem=sum_send.at[phase, which],
            recv_sem=sum_recv.at[phase, which],
            device_id=(s, lax.rem(r + 1, PEERS)),
            device_id_type=MESH,
        )

    def add_and_gather(which):
        pack, parts, mine, full, chunk = sums[which]
        place = pl.ds(pl.multiple_of(r * chunk, 8), chunk)
        arrived(0, which).wait_recv()
        total = pack[place, :]
        for i in range(PEERS - 1):
            total = total + parts[i]
        mine[...] = total
        full[place, :] = total

        def one(i, carry):
            pltpu.make_async_remote_copy(
                src_ref=mine,
                dst_ref=full.at[place, :],
                send_sem=sum_send.at[1, which],
                recv_sem=sum_recv.at[1, which],
                device_id=(s, lax.rem(r + i, PEERS)),
                device_id_type=MESH,
            ).start()
            return carry

        lax.fori_loop(1, PEERS, one, 0)

    gram = g_hh[...] + (g_hl[...] + g_hl[...].T)
    pack_g[0:W, :] = gram[:, 0:128]
    pack_g[W : W + 64, 0:64] = gram[128:W, 128:W]
    scatter(0)
    for c in range(CHUNKS // 2):
        pl.when(paced)(lambda c=c: exchange(1, c, 1).start())

    load_y.wait()

    def rest_step(c, carry):
        exchange(1, c, 0).wait_recv()
        blend(y, fi, near_row, c)
        high, low = split(y[pl.ds(rest_row, 128), lanes(c)])
        base = xh[:, lanes(c)]
        proj[0:128, :] += dot_rows(high, base) + (dot_rows(high, xl[:, lanes(c)]) + dot_rows(low, base))
        return carry

    lax.fori_loop(0, CHUNKS, rest_step, 0)
    pack_f[0:128, :] = proj[0:128, 0:128]
    pack_f[128:W, 0:64] = proj[0:64, 128:W]
    pack_f[128:W, 64:128] = proj[64:128, 128:W]
    add_and_gather(0)
    scatter(1)
    for c in range(CHUNKS // 2, CHUNKS):
        pl.when(paced)(lambda c=c: exchange(1, c, 1).start())

    def far_step(c, carry):
        @pl.when(has_slow)
        def _():
            exchange(1, c, 1).wait_recv()
            blend(y, si, far_row, c)

        high, low = split(y[pl.ds(far_row, SHARED), lanes(c)])
        base = xh[:, lanes(c)]
        proj[128:W, :] += dot_rows(high, base) + (dot_rows(high, xl[:, lanes(c)]) + dot_rows(low, base))
        return carry

    lax.fori_loop(0, CHUNKS // 2, far_step, 0)
    arrived(1, 0).wait_recv()
    a_ref[:, 0:128] = full_g[0:W, :]
    corner = jnp.concatenate([full_g[128:W, :].T, full_g[W : W + 64, 0:64]], 0)
    a_ref[:, 128:LANES] = jnp.concatenate([corner, jnp.zeros((W, 64), F32)], 1)
    lax.fori_loop(CHUNKS // 2, CHUNKS, far_step, 0)
    pack_s[0:64, :] = proj[128:W, 0:128]
    pack_s[64:128, 0:64] = proj[128:W, 128:W]
    scatter(2)

    def early(c):
        return pltpu.make_async_remote_copy(
            src_ref=x.at[0:128, lanes(c)],
            dst_ref=xp.at[:, lanes(c)],
            send_sem=fwd_send.at[c],
            recv_sem=fwd_recv.at[c],
            device_id=(upper, r),
            device_id_type=MESH,
        )

    @pl.when(has_upper)
    def _():
        early(0).start()

    def sweep_step(step, carry):
        sweep_panel(step, a_ref, p_ref, d_ref)
        return carry

    lax.fori_loop(0, 1, sweep_step, 0)
    add_and_gather(1)
    lax.fori_loop(1, 3, sweep_step, 0)
    add_and_gather(2)

    @pl.when(has_upper)
    def _():
        for c in range(1, EARLY):
            early(c).start()

    lax.fori_loop(3, W // PANEL, sweep_step, 0)

    arrived(1, 1).wait_recv()
    pt_ref[pl.ds(rest_row, 128), 0:128] = full_f[0:128, :]
    pt_ref[pl.ds(rest_row, 64), 128:W] = full_f[128:W, 0:64]
    pt_ref[pl.ds(rest_row + 64, 64), 128:W] = full_f[128:W, 64:128]
    arrived(1, 2).wait_recv()
    pt_ref[pl.ds(far_row, 64), 0:128] = full_s[0:64, :]
    pt_ref[pl.ds(far_row, 64), 128:W] = full_s[64:128, 0:64]
    coeff = dot(pt_ref[...], -a_ref[:, 0:W])
    passed = dot(select[KEEP_DEV:W, :], coeff)
    kn[...] = passed

    late = pltpu.make_async_remote_copy(
        src_ref=kn,
        dst_ref=kp,
        send_sem=fwd_send.at[CHUNKS],
        recv_sem=fwd_recv.at[CHUNKS],
        device_id=(upper, r),
        device_id_type=MESH,
    )

    def product(c):
        place = pl.ds(pl.multiple_of((c - EARLY) * CHUNK, CHUNK), CHUNK)
        return pltpu.make_async_remote_copy(
            src_ref=z_out.at[:, place],
            dst_ref=z_in.at[:, place],
            send_sem=fwd_send.at[c],
            recv_sem=fwd_recv.at[c],
            device_id=(upper, r),
            device_id_type=MESH,
        )

    @pl.when(has_upper)
    def _():
        late.start()
        factor = split(passed)

        def product_step(c, carry):
            z_out[:, pl.ds(pl.multiple_of((c - EARLY) * CHUNK, CHUNK), CHUNK)] = dot_split(
                factor, (xh[:, lanes(c)], xl[:, lanes(c)])
            )
            product(c).start()
            return carry

        lax.fori_loop(EARLY, CHUNKS, product_step, 0)

    high, low = split(coeff)
    lhs_h[0:W, :] = high
    lhs_l[0:W, :] = low
    high, low = split(dot(select[0:KEEP_DEV, :], coeff))
    lhs_h[W : W + KEEP_DEV, :] = high
    lhs_l[W : W + KEEP_DEV, :] = low

    def rotate_step(c, carry):
        both = dot_split((lhs_h[...], lhs_l[...]), (xh[:, lanes(c)], xl[:, lanes(c)]))
        res_ref[:, lanes(c)] = y[:, lanes(c)] - both[0:W]
        kept_ref[:, lanes(c)] = both[W : W + KEEP_DEV]
        return carry

    lax.fori_loop(0, CHUNKS, rotate_step, 0)

    @pl.when(has_lower)
    def _():
        late.wait_recv()
        first = split(kp[:, 0:128])
        last = split(kp[:, 128:W])

        def early_step(c, carry):
            early(c).wait_recv()
            extra = dot_split(first, split(xp[:, lanes(c)]))
            extra = extra + dot_split(last, (xh[0:SHARED, lanes(c)], xl[0:SHARED, lanes(c)]))
            kept_ref[:, lanes(c)] += extra
            return carry

        lax.fori_loop(0, EARLY, early_step, 0)

        def late_step(c, carry):
            product(c).wait_recv()
            kept_ref[:, lanes(c)] += z_in[:, pl.ds(pl.multiple_of((c - EARLY) * CHUNK, CHUNK), CHUNK)]
            return carry

        lax.fori_loop(EARLY, CHUNKS, late_step, 0)

    for kind in range(2):
        for c in range(CHUNKS):
            exchange(kind, c, 0).wait_send()
            when_slow(lambda kind=kind, c=c: exchange(kind, c, 1).wait_send())
    for phase in range(2):
        for which in range(3):
            arrived(phase, which).wait_send()

    @pl.when(has_upper)
    def _():
        late.wait_send()
        for c in range(EARLY):
            early(c).wait_send()
        for c in range(EARLY, CHUNKS):
            product(c).wait_send()


def fused_call(vectors, images, flags):
    shape = jax.ShapeDtypeStruct
    dma = pltpu.SemaphoreType.DMA

    def vmem(*dims, dtype=F32):
        return pltpu.VMEM(dims, dtype)

    big, shared = vmem(W, ROWS), vmem(SHARED, ROWS)
    half = vmem(W, ROWS, dtype=BF16)
    late_rows = vmem(KEEP_DEV, ROWS - EARLY_ROWS)
    chunks = [size // PEERS for size in PACK]
    return pl.pallas_call(
        fused_kernel,
        out_shape=(shape((W, ROWS), F32), shape((KEEP_DEV, ROWS), F32)),
        in_specs=[HBM, HBM, VMEM],
        out_specs=(VMEM, VMEM),
        scratch_shapes=[
            big, big, half, half, shared, shared, shared, shared,
            vmem(2 * SHARED, EARLY_ROWS), late_rows, late_rows,
            vmem(W, W), vmem(W, W), vmem(W, W),
            *[vmem(size, 128) for size in PACK],
            *[vmem(PEERS - 1, chunk, 128) for chunk in chunks],
            *[vmem(chunk, 128) for chunk in chunks],
            *[vmem(size, 128) for size in PACK],
            vmem(W, LANES), vmem(PANEL, LANES), vmem(8, 8, 128), vmem(W, W), vmem(W, W), vmem(KEEP_DEV, W), vmem(KEEP_DEV, W),
            vmem(W + KEEP_DEV, W, dtype=BF16), vmem(W + KEEP_DEV, W, dtype=BF16),
            dma((2,)), dma((2, 2, CHUNKS)), dma((2, 2, CHUNKS)), dma((2, 3)), dma((2, 3)),
            dma((CHUNKS + 1,)), dma((CHUNKS + 1,)),
        ],
        compiler_params=pltpu.CompilerParams(
            collective_id=0, has_side_effects=True, vmem_limit_bytes=VMEM_LIMIT
        ),
        name="fused",
    )(vectors, images, flags)


def on_device(vectors, images, kept_flags):
    residual, kept = fused_call(vectors[0].T, images[0].T, kept_flags)
    return residual.T[None], kept.T[None]


def solution(mesh):
    placed = (P("cuts", "row", None), P("cuts", "row", None), P())
    return jax.shard_map(
        on_device,
        mesh=mesh,
        in_specs=placed,
        out_specs=(P("cuts", "row", None), P("cuts", "row", None)),
        check_vma=False,
    )
```

```python
import functools

import jax
import jax.numpy as jnp
from jax import lax
from jax.experimental import pallas as pl
from jax.experimental.pallas import tpu as pltpu
from jax.sharding import PartitionSpec as P

W = 192
SHARED = 64
KEEP_DEV = 96
SLICES = 16
ROWS = 4096
PEERS = 16
DEPTH = 8
CHUNKS = 4
CHUNK = ROWS // CHUNKS
UNITS = 8
UNIT = ROWS // UNITS
FIRST = 2
EARLY = 6
EARLY_ROWS = EARLY * UNIT
LANES = 256
PANEL = 48
VMEM_LIMIT = 48 << 20
PACK = (192, 192, 128)
F32 = jnp.float32
BF16 = jnp.bfloat16
HIGH = lax.Precision.HIGHEST
MESH = pl.DeviceIdType.MESH
HBM = pl.BlockSpec(memory_space=pltpu.HBM)
VMEM = pl.BlockSpec(memory_space=pltpu.VMEM)


def split(a):
    high = a.astype(BF16)
    return high, (a - high.astype(F32)).astype(BF16)


def dot_rows(a, b):
    return lax.dot_general(a, b, (((1,), (1,)), ((), ())), preferred_element_type=F32)


def dot_split(a, b):
    def one(x, y):
        return lax.dot_general(x, y, (((1,), (0,)), ((), ())), preferred_element_type=F32)

    return one(a[0], b[0]) + (one(a[0], b[1]) + one(a[1], b[0]))


def dot(a, b):
    return lax.dot_general(a, b, (((1,), (0,)), ((), ())), precision=HIGH, preferred_element_type=F32)


def sweep_block(kb, q, p_ref, d_ref):
    base = kb * 8
    first = 8 * q
    lane = lax.broadcasted_iota(jnp.int32, (8, LANES), 1) - base
    in_block = jnp.logical_and(lane >= 0, lane < 8)
    half = pl.ds(pl.multiple_of((kb // 16) * 128, 128), 128)
    turn = lax.rem(128 - lax.rem(base, 128), 128)
    pivots = {z: pltpu.roll(p_ref[8 * z : 8 * z + 8, half], turn, 1) for z in range(PANEL // 8)}
    for j in range(8):
        d_ref[j] = jnp.broadcast_to(pivots[q][:, j : j + 1], (8, 128))
    d = {}
    for i in range(8):
        for j in range(i, 8):
            d[i, j] = jnp.broadcast_to(d_ref[j, i : i + 1, :], (8, 128))

    def at(i, j):
        return d[min(i, j), max(i, j)]

    for k in range(8):
        pivot = 1.0 / d[k, k]
        scaled = {i: at(i, k) * pivot for i in range(8) if i != k}
        for i in range(8):
            for j in range(i, 8):
                if i != k and j != k:
                    d[i, j] = d[i, j] - scaled[i] * at(j, k)
        for i in range(8):
            if i != k:
                d[min(i, k), max(i, k)] = scaled[i]
        d[k, k] = -pivot
    rows = []
    for j in range(8):
        row = jnp.broadcast_to(p_ref[first + j : first + j + 1, :], (8, LANES))
        rows.append(jnp.where(in_block, jnp.where(lane == j, 1.0, 0.0), -row))
    solved = []
    for i in range(8):
        total = None
        for j in range(8):
            term = jnp.concatenate([at(i, j)] * 2, 1) * rows[j]
            total = term if total is None else total + term
        solved.append(total)
    for z in range(PANEL // 8):
        if z != q:
            total = jnp.where(in_block, 0.0, p_ref[8 * z : 8 * z + 8, :])
            for j in range(8):
                total = total - jnp.broadcast_to(pivots[z][:, j : j + 1], (8, LANES)) * solved[j]
            p_ref[8 * z : 8 * z + 8, :] = total
    sublane = lax.broadcasted_iota(jnp.int32, (8, LANES), 0)
    mine = solved[0]
    for i in range(1, 8):
        mine = jnp.where(sublane == i, solved[i], mine)
    p_ref[first : first + 8, :] = mine


def sweep_panel(step, a_ref, p_ref, d_ref):
    base = pl.multiple_of(step * PANEL, PANEL)
    panel = a_ref[pl.ds(base, PANEL), :]
    p_ref[...] = panel
    for q in range(PANEL // 8):
        sweep_block(step * (PANEL // 8) + q, q, p_ref, d_ref)
    swept = p_ref[...]
    update = lax.dot_general(
        panel[:, 0:W], swept, (((0,), (0,)), ((), ())), precision=HIGH, preferred_element_type=F32
    )
    lane = lax.broadcasted_iota(jnp.int32, (W, LANES), 1) - base
    a_ref[...] = jnp.where(jnp.logical_and(lane >= 0, lane < PANEL), 0.0, a_ref[...]) - update
    a_ref[pl.ds(base, PANEL), :] = swept


def fused_kernel(
    v_hbm, i_hbm, flags_ref,
    res_ref, kept_ref,
    x, y, xh, xl, fv, fi, sv, si, xp, z_out, z_in, g_hh, g_hl, proj,
    pack_g, pack_f, pack_s, parts_g, parts_f, parts_s, mine_g, mine_f, mine_s, full_g, full_f, full_s,
    other_g, other_f,
    a_ref, p_ref, d_ref, pt_ref, select, kn, kp, lhs_h, lhs_l,
    load_sem, ex_send, ex_recv, sum_send, sum_recv, fwd_send, fwd_recv,
):
    s = lax.axis_index("cuts")
    r = lax.axis_index("row")
    odd = lax.rem(s, 2)
    has_lower = s > 0
    has_upper = s < SLICES - 1
    has_slow = jnp.logical_and(has_lower, has_upper)
    upper = lax.rem(s + 1, SLICES)
    near = s + 1 - 2 * odd
    far = lax.rem(s + SLICES - 1 + 2 * odd, SLICES)
    near_row = pl.multiple_of(128 - 128 * odd, 64)
    far_row = pl.multiple_of(128 * odd, 64)
    rest_row = pl.multiple_of(64 - 64 * odd, 64)

    load_x = pltpu.make_async_copy(v_hbm, x, load_sem.at[0])
    load_y = pltpu.make_async_copy(i_hbm, y, load_sem.at[1])
    load_x.start()
    load_y.start()

    barrier = pltpu.get_barrier_semaphore()
    for q in (near, far):
        pl.semaphore_signal(barrier, inc=1, device_id=(q, r), device_id_type=MESH)

    def greet(i, carry):
        pl.semaphore_signal(barrier, inc=1, device_id=(s, lax.rem(r + i, PEERS)), device_id_type=MESH)
        return carry

    lax.fori_loop(1, PEERS, greet, 0)

    flags = flags_ref[...].astype(F32)
    row_id = lax.broadcasted_iota(jnp.int32, (SLICES, W), 0)
    before = jnp.sum(jnp.where(row_id < s, flags, 0.0), keepdims=True)
    own_flags = jnp.sum(jnp.where(row_id == s, flags, 0.0), axis=0, keepdims=True)
    earlier = lax.broadcasted_iota(jnp.int32, (W, W), 0) < lax.broadcasted_iota(jnp.int32, (W, W), 1)
    ranks = dot(jnp.broadcast_to(own_flags, (8, W)), jnp.where(earlier, 1.0, 0.0))[0:1]
    slot = ranks + before - (s * KEEP_DEV).astype(F32)
    slot_id = lax.broadcasted_iota(jnp.int32, (W, W), 0).astype(F32)
    select[...] = jnp.where(jnp.logical_and(slot_id == slot, own_flags > 0.5), 1.0, 0.0)
    for ref in (g_hh, g_hl, proj, pack_s):
        ref[...] = jnp.zeros_like(ref)

    pl.semaphore_wait(barrier, PEERS + 1)

    def lanes(c):
        return pl.ds(pl.multiple_of(c * CHUNK, CHUNK), CHUNK)

    def unit(c):
        return pl.ds(pl.multiple_of(c * UNIT, UNIT), UNIT)

    def exchange(kind, c, way):
        return pltpu.make_async_remote_copy(
            src_ref=(v_hbm, i_hbm)[kind].at[pl.ds((near_row, far_row)[way], SHARED), lanes(c)],
            dst_ref=((fv, sv), (fi, si))[kind][way].at[:, lanes(c)],
            send_sem=ex_send.at[kind, way, c],
            recv_sem=ex_recv.at[kind, way, c],
            device_id=((near, far)[way], r),
            device_id_type=MESH,
        )

    def when_slow(action):
        pl.when(has_slow)(action)

    def blend(own, other, row, c):
        mine = own[pl.ds(row, SHARED), lanes(c)]
        own[pl.ds(row, SHARED), lanes(c)] = 0.5 * (mine + other[:, lanes(c)])

    for c in range(CHUNKS):
        when_slow(lambda c=c: exchange(0, c, 1).start())
        exchange(0, c, 0).start()
    for c in range(CHUNKS):
        exchange(1, c, 0).start()
    when_slow(lambda: exchange(1, 0, 1).start())
    load_x.wait()
    load_y.wait()

    def gram_step(c, carry):
        exchange(0, c, 0).wait_recv()
        blend(x, fv, near_row, c)

        @pl.when(has_slow)
        def _():
            exchange(0, c, 1).wait_recv()
            blend(x, sv, far_row, c)

        high, low = split(x[:, lanes(c)])
        xh[:, lanes(c)] = high
        xl[:, lanes(c)] = low
        g_hh[...] += dot_rows(high, high)
        g_hl[...] += dot_rows(high, low)

        exchange(1, c, 0).wait_recv()
        blend(y, fi, near_row, c)
        rest_high, rest_low = split(y[pl.ds(rest_row, 128), lanes(c)])
        proj[0:128, :] += dot_rows(rest_high, high) + (dot_rows(rest_high, low) + dot_rows(rest_low, high))
        return carry

    lax.fori_loop(0, CHUNKS, gram_step, 0)
    sums = (
        (pack_g, parts_g, mine_g, full_g, other_g, PACK[0] // DEPTH),
        (pack_f, parts_f, mine_f, full_f, other_f, PACK[1] // DEPTH),
        (pack_s, parts_s, mine_s, full_s, None, PACK[2] // DEPTH),
    )
    partner = r + 1 - 2 * lax.rem(r, 2)

    def along_z(i):
        return lax.rem(r + 2 * i, PEERS)

    def swap(which):
        pack, _, _, _, other, _ = sums[which]
        return pltpu.make_async_remote_copy(
            src_ref=pack,
            dst_ref=other,
            send_sem=sum_send.at[2, which],
            recv_sem=sum_recv.at[2, which],
            device_id=(s, partner),
            device_id_type=MESH,
        )

    def scatter(which):
        pack, parts, _, _, other, chunk = sums[which]
        if which < 2:
            swap(which).wait()
            pack[...] += other[...]

        def one(i, carry):
            q = along_z(i) if which < 2 else lax.rem(r + i, PEERS)
            pltpu.make_async_remote_copy(
                src_ref=pack.at[pl.ds(pl.multiple_of((q // 2) * chunk, 8), chunk), :],
                dst_ref=parts.at[i - 1],
                send_sem=sum_send.at[0, which],
                recv_sem=sum_recv.at[0, which],
                device_id=(s, q),
                device_id_type=MESH,
            ).start()
            return carry

        lax.fori_loop(1, DEPTH if which < 2 else PEERS, one, 0)

    def arrived(phase, which):
        parts = sums[which][1]
        if phase == 1:
            parts = parts.at[0 : DEPTH - 1]
        return pltpu.make_async_remote_copy(
            src_ref=parts,
            dst_ref=parts,
            send_sem=sum_send.at[phase, which],
            recv_sem=sum_recv.at[phase, which],
            device_id=(s, along_z(1)),
            device_id_type=MESH,
        )

    def add_and_gather(which):
        pack, parts, mine, full, _, chunk = sums[which]
        place = pl.ds(pl.multiple_of((r // 2) * chunk, 8), chunk)
        arrived(0, which).wait_recv()
        total = pack[place, :]
        for i in range(DEPTH - 1 if which < 2 else PEERS - 1):
            total = total + parts[i]
        mine[...] = total
        full[place, :] = total

        def one(i, carry):
            pltpu.make_async_remote_copy(
                src_ref=mine,
                dst_ref=full.at[place, :],
                send_sem=sum_send.at[1, which],
                recv_sem=sum_recv.at[1, which],
                device_id=(s, along_z(i)),
                device_id_type=MESH,
            ).start()
            return carry

        lax.fori_loop(1, DEPTH, one, 0)

    gram = g_hh[...] + (g_hl[...] + g_hl[...].T)
    pack_g[:, 0:64] = gram[:, 0:64]
    pack_g[64:W, 64:128] = gram[64:W, 64:128]
    pack_g[0:64, 64:128] = gram[128:W, 128:W]
    swap(0).start()
    pack_f[0:128, :] = proj[0:128, 0:128]
    pack_f[128:W, 0:64] = proj[0:64, 128:W]
    pack_f[128:W, 64:128] = proj[64:128, 128:W]
    swap(1).start()
    for c in range(1, CHUNKS):
        when_slow(lambda c=c: exchange(1, c, 1).start())

    def early(c):
        return pltpu.make_async_remote_copy(
            src_ref=x.at[0:128, unit(c)],
            dst_ref=xp.at[:, unit(c)],
            send_sem=fwd_send.at[c],
            recv_sem=fwd_recv.at[c],
            device_id=(upper, r),
            device_id_type=MESH,
        )

    @pl.when(has_upper)
    def _():
        for c in range(FIRST):
            early(c).start()

    scatter(0)
    scatter(1)
    add_and_gather(0)
    add_and_gather(1)

    def far_step(c, carry):
        @pl.when(has_slow)
        def _():
            exchange(1, c, 1).wait_recv()
            blend(y, si, far_row, c)

        high, low = split(y[pl.ds(far_row, SHARED), lanes(c)])
        base = xh[:, lanes(c)]
        proj[128:W, :] += dot_rows(high, base) + (dot_rows(high, xl[:, lanes(c)]) + dot_rows(low, base))
        return carry

    lax.fori_loop(0, CHUNKS // 2, far_step, 0)
    arrived(1, 0).wait_recv()
    a_ref[64:W, 0:128] = full_g[64:W, :]
    a_ref[0:64, 0:128] = jnp.concatenate([full_g[0:64, 0:64], full_g[64:128, 0:64].T], 1)
    corner = jnp.concatenate([full_g[128:W, :].T, full_g[0:64, 64:128]], 0)
    a_ref[:, 128:LANES] = jnp.concatenate([corner, jnp.zeros((W, 64), F32)], 1)
    lax.fori_loop(CHUNKS // 2, CHUNKS, far_step, 0)
    pack_s[0:64, :] = proj[128:W, 0:128]
    pack_s[64:128, 0:64] = proj[128:W, 128:W]
    scatter(2)

    @pl.when(has_upper)
    def _():
        for c in range(FIRST, EARLY):
            early(c).start()

    def sweep_step(step, carry):
        sweep_panel(step, a_ref, p_ref, d_ref)
        return carry

    lax.fori_loop(0, 2, sweep_step, 0)
    add_and_gather(2)
    lax.fori_loop(2, W // PANEL, sweep_step, 0)

    arrived(1, 1).wait_recv()
    pt_ref[pl.ds(rest_row, 128), 0:128] = full_f[0:128, :]
    pt_ref[pl.ds(rest_row, 64), 128:W] = full_f[128:W, 0:64]
    pt_ref[pl.ds(rest_row + 64, 64), 128:W] = full_f[128:W, 64:128]
    arrived(1, 2).wait_recv()
    pt_ref[pl.ds(far_row, 64), 0:128] = full_s[0:64, :]
    pt_ref[pl.ds(far_row, 64), 128:W] = full_s[64:128, 0:64]
    coeff = dot(pt_ref[...], -a_ref[:, 0:W])
    passed = dot(select[KEEP_DEV:W, :], coeff)
    kn[...] = passed

    late = pltpu.make_async_remote_copy(
        src_ref=kn,
        dst_ref=kp,
        send_sem=fwd_send.at[UNITS],
        recv_sem=fwd_recv.at[UNITS],
        device_id=(upper, r),
        device_id_type=MESH,
    )

    def product(c):
        place = unit(c - EARLY)
        return pltpu.make_async_remote_copy(
            src_ref=z_out.at[:, place],
            dst_ref=z_in.at[:, place],
            send_sem=fwd_send.at[c],
            recv_sem=fwd_recv.at[c],
            device_id=(upper, r),
            device_id_type=MESH,
        )

    @pl.when(has_upper)
    def _():
        late.start()
        factor = split(passed)

        def product_step(c, carry):
            z_out[:, unit(c - EARLY)] = dot_split(factor, (xh[:, unit(c)], xl[:, unit(c)]))
            product(c).start()
            return carry

        lax.fori_loop(EARLY, UNITS, product_step, 0)

    high, low = split(coeff)
    lhs_h[0:W, :] = high
    lhs_l[0:W, :] = low
    high, low = split(dot(select[0:KEEP_DEV, :], coeff))
    lhs_h[W : W + KEEP_DEV, :] = high
    lhs_l[W : W + KEEP_DEV, :] = low

    def rotate_step(c, carry):
        both = dot_split((lhs_h[...], lhs_l[...]), (xh[:, lanes(c)], xl[:, lanes(c)]))
        res_ref[:, lanes(c)] = y[:, lanes(c)] - both[0:W]
        kept_ref[:, lanes(c)] = both[W : W + KEEP_DEV]
        return carry

    lax.fori_loop(0, CHUNKS, rotate_step, 0)

    @pl.when(has_lower)
    def _():
        late.wait_recv()
        first = split(kp[:, 0:128])
        last = split(kp[:, 128:W])

        def early_step(c, carry):
            early(c).wait_recv()
            extra = dot_split(first, split(xp[:, unit(c)]))
            extra = extra + dot_split(last, (xh[0:SHARED, unit(c)], xl[0:SHARED, unit(c)]))
            kept_ref[:, unit(c)] += extra
            return carry

        lax.fori_loop(0, EARLY, early_step, 0)

        def late_step(c, carry):
            product(c).wait_recv()
            kept_ref[:, unit(c)] += z_in[:, unit(c - EARLY)]
            return carry

        lax.fori_loop(EARLY, UNITS, late_step, 0)

    for kind in range(2):
        for c in range(CHUNKS):
            exchange(kind, c, 0).wait_send()
            when_slow(lambda kind=kind, c=c: exchange(kind, c, 1).wait_send())
    for phase in range(2):
        for which in range(3):
            arrived(phase, which).wait_send()

    @pl.when(has_upper)
    def _():
        late.wait_send()
        for c in range(EARLY):
            early(c).wait_send()
        for c in range(EARLY, UNITS):
            product(c).wait_send()


def fused_call(vectors, images, flags):
    shape = jax.ShapeDtypeStruct
    dma = pltpu.SemaphoreType.DMA

    def vmem(*dims, dtype=F32):
        return pltpu.VMEM(dims, dtype)

    big, shared = vmem(W, ROWS), vmem(SHARED, ROWS)
    half = vmem(W, ROWS, dtype=BF16)
    late_rows = vmem(KEEP_DEV, ROWS - EARLY_ROWS)
    chunks = [size // DEPTH for size in PACK]
    return pl.pallas_call(
        fused_kernel,
        out_shape=(shape((W, ROWS), F32), shape((KEEP_DEV, ROWS), F32)),
        in_specs=[HBM, HBM, VMEM],
        out_specs=(VMEM, VMEM),
        scratch_shapes=[
            big, big, half, half, shared, shared, shared, shared,
            vmem(2 * SHARED, EARLY_ROWS), late_rows, late_rows,
            vmem(W, W), vmem(W, W), vmem(W, W),
            *[vmem(size, 128) for size in PACK],
            *[vmem(count - 1, chunk, 128) for count, chunk in zip((DEPTH, DEPTH, PEERS), chunks)],
            *[vmem(chunk, 128) for chunk in chunks],
            *[vmem(size, 128) for size in PACK],
            *[vmem(size, 128) for size in PACK[0:2]],
            vmem(W, LANES), vmem(PANEL, LANES), vmem(8, 8, 128), vmem(W, W), vmem(W, W), vmem(KEEP_DEV, W), vmem(KEEP_DEV, W),
            vmem(W + KEEP_DEV, W, dtype=BF16), vmem(W + KEEP_DEV, W, dtype=BF16),
            dma((2,)), dma((2, 2, CHUNKS)), dma((2, 2, CHUNKS)), dma((3, 3)), dma((3, 3)),
            dma((UNITS + 1,)), dma((UNITS + 1,)),
        ],
        compiler_params=pltpu.CompilerParams(
            collective_id=0, has_side_effects=True, vmem_limit_bytes=VMEM_LIMIT
        ),
        name="fused",
    )(vectors, images, flags)


def on_device(vectors, images, kept_flags):
    residual, kept = fused_call(vectors[0].T, images[0].T, kept_flags)
    return residual.T[None], kept.T[None]


def solution(mesh):
    placed = (P("cuts", "row", None), P("cuts", "row", None), P())
    return jax.shard_map(
        on_device,
        mesh=mesh,
        in_specs=placed,
        out_specs=(P("cuts", "row", None), P("cuts", "row", None)),
        check_vma=False,
    )
```

```python
import functools

import jax
import jax.numpy as jnp
from jax import lax
from jax.experimental import pallas as pl
from jax.experimental.pallas import tpu as pltpu
from jax.sharding import PartitionSpec as P

W = 192
SHARED = 64
KEEP_DEV = 96
SLICES = 16
ROWS = 4096
PEERS = 16
DEPTH = 8
CHUNKS = 4
CHUNK = ROWS // CHUNKS
UNITS = 8
UNIT = ROWS // UNITS
FIRST = 3
EARLY = 7
RELAYED = 4
SOURCE = SLICES // 2 - 1
TARGET = SLICES // 2
EARLY_ROWS = EARLY * UNIT
LANES = 256
PANEL = 48
VMEM_LIMIT = 48 << 20
PACK = (192, 192, 128)
F32 = jnp.float32
BF16 = jnp.bfloat16
HIGH = lax.Precision.HIGHEST
MESH = pl.DeviceIdType.MESH
HBM = pl.BlockSpec(memory_space=pltpu.HBM)
VMEM = pl.BlockSpec(memory_space=pltpu.VMEM)


def split(a):
    high = a.astype(BF16)
    return high, (a - high.astype(F32)).astype(BF16)


def dot_rows(a, b):
    return lax.dot_general(a, b, (((1,), (1,)), ((), ())), preferred_element_type=F32)


def dot_split(a, b):
    def one(x, y):
        return lax.dot_general(x, y, (((1,), (0,)), ((), ())), preferred_element_type=F32)

    return one(a[0], b[0]) + (one(a[0], b[1]) + one(a[1], b[0]))


def dot(a, b):
    return lax.dot_general(a, b, (((1,), (0,)), ((), ())), precision=HIGH, preferred_element_type=F32)


def sweep_block(kb, q, p_ref, d_ref):
    base = kb * 8
    first = 8 * q
    lane = lax.broadcasted_iota(jnp.int32, (8, LANES), 1) - base
    in_block = jnp.logical_and(lane >= 0, lane < 8)
    half = pl.ds(pl.multiple_of((kb // 16) * 128, 128), 128)
    turn = lax.rem(128 - lax.rem(base, 128), 128)
    pivots = {z: pltpu.roll(p_ref[8 * z : 8 * z + 8, half], turn, 1) for z in range(PANEL // 8)}
    for j in range(8):
        d_ref[j] = jnp.broadcast_to(pivots[q][:, j : j + 1], (8, 128))
    d = {}
    for i in range(8):
        for j in range(i, 8):
            d[i, j] = jnp.broadcast_to(d_ref[j, i : i + 1, :], (8, 128))

    def at(i, j):
        return d[min(i, j), max(i, j)]

    for k in range(8):
        pivot = 1.0 / d[k, k]
        scaled = {i: at(i, k) * pivot for i in range(8) if i != k}
        for i in range(8):
            for j in range(i, 8):
                if i != k and j != k:
                    d[i, j] = d[i, j] - scaled[i] * at(j, k)
        for i in range(8):
            if i != k:
                d[min(i, k), max(i, k)] = scaled[i]
        d[k, k] = -pivot
    rows = []
    for j in range(8):
        row = jnp.broadcast_to(p_ref[first + j : first + j + 1, :], (8, LANES))
        rows.append(jnp.where(in_block, jnp.where(lane == j, 1.0, 0.0), -row))
    solved = []
    for i in range(8):
        total = None
        for j in range(8):
            term = jnp.concatenate([at(i, j)] * 2, 1) * rows[j]
            total = term if total is None else total + term
        solved.append(total)
    for z in range(PANEL // 8):
        if z != q:
            total = jnp.where(in_block, 0.0, p_ref[8 * z : 8 * z + 8, :])
            for j in range(8):
                total = total - jnp.broadcast_to(pivots[z][:, j : j + 1], (8, LANES)) * solved[j]
            p_ref[8 * z : 8 * z + 8, :] = total
    sublane = lax.broadcasted_iota(jnp.int32, (8, LANES), 0)
    mine = solved[0]
    for i in range(1, 8):
        mine = jnp.where(sublane == i, solved[i], mine)
    p_ref[first : first + 8, :] = mine


def sweep_panel(step, a_ref, p_ref, d_ref):
    base = pl.multiple_of(step * PANEL, PANEL)
    panel = a_ref[pl.ds(base, PANEL), :]
    p_ref[...] = panel
    for q in range(PANEL // 8):
        sweep_block(step * (PANEL // 8) + q, q, p_ref, d_ref)
    swept = p_ref[...]
    update = lax.dot_general(
        panel[:, 0:W], swept, (((0,), (0,)), ((), ())), precision=HIGH, preferred_element_type=F32
    )
    lane = lax.broadcasted_iota(jnp.int32, (W, LANES), 1) - base
    a_ref[...] = jnp.where(jnp.logical_and(lane >= 0, lane < PANEL), 0.0, a_ref[...]) - update
    a_ref[pl.ds(base, PANEL), :] = swept


def fused_kernel(
    v_hbm, i_hbm, flags_ref,
    res_ref, kept_ref,
    x, y, xh, xl, fv, fi, sv, si, xp, z_out, z_in, g_hh, g_hl, proj,
    pack_g, pack_f, pack_s, parts_g, parts_f, parts_s, mine_g, mine_f, mine_s, full_g, full_f, full_s,
    other_g, other_f,
    a_ref, p_ref, d_ref, pt_ref, select, kn, kp, lhs_h, lhs_l,
    load_sem, ex_send, ex_recv, sum_send, sum_recv, fwd_send, fwd_recv, relay_send,
):
    s = lax.axis_index("cuts")
    r = lax.axis_index("row")
    odd = lax.rem(s, 2)
    has_lower = s > 0
    has_upper = s < SLICES - 1
    has_slow = jnp.logical_and(has_lower, has_upper)
    upper = lax.rem(s + 1, SLICES)
    near = s + 1 - 2 * odd
    far = lax.rem(s + SLICES - 1 + 2 * odd, SLICES)
    near_row = pl.multiple_of(128 - 128 * odd, 64)
    far_row = pl.multiple_of(128 * odd, 64)
    rest_row = pl.multiple_of(64 - 64 * odd, 64)

    load_x = pltpu.make_async_copy(v_hbm, x, load_sem.at[0])
    load_y = pltpu.make_async_copy(i_hbm, y, load_sem.at[1])
    load_x.start()
    load_y.start()

    barrier = pltpu.get_barrier_semaphore()
    for q in (near, far):
        pl.semaphore_signal(barrier, inc=1, device_id=(q, r), device_id_type=MESH)

    def greet(i, carry):
        pl.semaphore_signal(barrier, inc=1, device_id=(s, lax.rem(r + i, PEERS)), device_id_type=MESH)
        return carry

    lax.fori_loop(1, PEERS, greet, 0)

    is_source = s == SOURCE
    at_ends = jnp.logical_or(is_source, s == TARGET)

    @pl.when(s == 0)
    def _():
        for q in (SOURCE, TARGET):
            pl.semaphore_signal(barrier, inc=1, device_id=(q, r), device_id_type=MESH)

    @pl.when(at_ends)
    def _():
        pl.semaphore_signal(barrier, inc=1, device_id=(0, r), device_id_type=MESH)


    pl.semaphore_wait(barrier, PEERS + 1 + jnp.where(s == 0, 2, jnp.where(at_ends, 1, 0)))

    def lanes(c):
        return pl.ds(pl.multiple_of(c * CHUNK, CHUNK), CHUNK)

    def unit(c):
        return pl.ds(pl.multiple_of(c * UNIT, UNIT), UNIT)

    def exchange(kind, c, way):
        return pltpu.make_async_remote_copy(
            src_ref=(v_hbm, i_hbm)[kind].at[pl.ds((near_row, far_row)[way], SHARED), lanes(c)],
            dst_ref=((fv, sv), (fi, si))[kind][way].at[:, lanes(c)],
            send_sem=ex_send.at[kind, way, c],
            recv_sem=ex_recv.at[kind, way, c],
            device_id=((near, far)[way], r),
            device_id_type=MESH,
        )

    def when_slow(action):
        pl.when(has_slow)(action)

    def blend(own, other, row, c):
        mine = own[pl.ds(row, SHARED), lanes(c)]
        own[pl.ds(row, SHARED), lanes(c)] = 0.5 * (mine + other[:, lanes(c)])

    for c in range(CHUNKS):
        when_slow(lambda c=c: exchange(0, c, 1).start())
        exchange(0, c, 0).start()
    for c in range(CHUNKS):
        exchange(1, c, 0).start()
    when_slow(lambda: exchange(1, 0, 1).start())

    flags = flags_ref[...].astype(F32)
    row_id = lax.broadcasted_iota(jnp.int32, (SLICES, W), 0)
    before = jnp.sum(jnp.where(row_id < s, flags, 0.0), keepdims=True)
    own_flags = jnp.sum(jnp.where(row_id == s, flags, 0.0), axis=0, keepdims=True)
    earlier = lax.broadcasted_iota(jnp.int32, (W, W), 0) < lax.broadcasted_iota(jnp.int32, (W, W), 1)
    ranks = dot(jnp.broadcast_to(own_flags, (8, W)), jnp.where(earlier, 1.0, 0.0))[0:1]
    slot = ranks + before - (s * KEEP_DEV).astype(F32)
    slot_id = lax.broadcasted_iota(jnp.int32, (W, W), 0).astype(F32)
    select[...] = jnp.where(jnp.logical_and(slot_id == slot, own_flags > 0.5), 1.0, 0.0)
    for ref in (g_hh, g_hl, proj, pack_s):
        ref[...] = jnp.zeros_like(ref)

    load_x.wait()
    load_y.wait()

    def gram_step(c, carry):
        exchange(0, c, 0).wait_recv()
        blend(x, fv, near_row, c)

        @pl.when(has_slow)
        def _():
            exchange(0, c, 1).wait_recv()
            blend(x, sv, far_row, c)

        high, low = split(x[:, lanes(c)])
        xh[:, lanes(c)] = high
        xl[:, lanes(c)] = low
        g_hh[...] += dot_rows(high, high)
        g_hl[...] += dot_rows(high, low)

        exchange(1, c, 0).wait_recv()
        blend(y, fi, near_row, c)
        rest_high, rest_low = split(y[pl.ds(rest_row, 128), lanes(c)])
        proj[0:128, :] += dot_rows(rest_high, high) + (dot_rows(rest_high, low) + dot_rows(rest_low, high))
        return carry

    lax.fori_loop(0, CHUNKS, gram_step, 0)
    sums = (
        (pack_g, parts_g, mine_g, full_g, other_g, PACK[0] // DEPTH),
        (pack_f, parts_f, mine_f, full_f, other_f, PACK[1] // DEPTH),
        (pack_s, parts_s, mine_s, full_s, None, PACK[2] // DEPTH),
    )
    partner = r + 1 - 2 * lax.rem(r, 2)

    def along_z(i):
        return lax.rem(r + 2 * i, PEERS)

    def swap(which):
        pack, _, mine, _, other, _ = sums[which]
        return pltpu.make_async_remote_copy(
            src_ref=(pack, mine)[which],
            dst_ref=other,
            send_sem=sum_send.at[2, which],
            recv_sem=sum_recv.at[2, which],
            device_id=(s, partner),
            device_id_type=MESH,
        )

    def scatter(which):
        pack, parts, _, _, other, chunk = sums[which]
        if which == 0:
            swap(0).wait()
            pack[...] += other[...]

        def one(i, carry):
            q = along_z(i) if which < 2 else lax.rem(r + i, PEERS)
            pltpu.make_async_remote_copy(
                src_ref=pack.at[pl.ds(pl.multiple_of((q // 2) * chunk, 8), chunk), :],
                dst_ref=parts.at[i - 1],
                send_sem=sum_send.at[0, which],
                recv_sem=sum_recv.at[0, which],
                device_id=(s, q),
                device_id_type=MESH,
            ).start()
            return carry

        lax.fori_loop(1, DEPTH if which < 2 else PEERS, one, 0)

    def arrived(phase, which):
        parts = sums[which][1]
        if phase == 1:
            parts = parts.at[0 : DEPTH - 1]
        return pltpu.make_async_remote_copy(
            src_ref=parts,
            dst_ref=parts,
            send_sem=sum_send.at[phase, which],
            recv_sem=sum_recv.at[phase, which],
            device_id=(s, along_z(1)),
            device_id_type=MESH,
        )

    def add_up(which):
        pack, parts, mine, _, _, chunk = sums[which]
        arrived(0, which).wait_recv()
        total = pack[pl.ds(pl.multiple_of((r // 2) * chunk, 8), chunk), :]
        for i in range(DEPTH - 1 if which < 2 else PEERS - 1):
            total = total + parts[i]
        mine[...] = total

    def gather(which):
        _, _, mine, full, _, chunk = sums[which]
        place = pl.ds(pl.multiple_of((r // 2) * chunk, 8), chunk)
        full[place, :] = mine[...]

        def one(i, carry):
            pltpu.make_async_remote_copy(
                src_ref=mine,
                dst_ref=full.at[place, :],
                send_sem=sum_send.at[1, which],
                recv_sem=sum_recv.at[1, which],
                device_id=(s, along_z(i)),
                device_id_type=MESH,
            ).start()
            return carry

        lax.fori_loop(1, DEPTH, one, 0)

    gram = g_hh[...] + (g_hl[...] + g_hl[...].T)
    pack_g[:, 0:64] = gram[:, 0:64]
    pack_g[64:W, 64:128] = gram[64:W, 64:128]
    pack_g[0:64, 64:128] = gram[128:W, 128:W]
    swap(0).start()
    pack_f[0:128, :] = proj[0:128, 0:128]
    pack_f[128:W, 0:64] = proj[0:64, 128:W]
    pack_f[128:W, 64:128] = proj[64:128, 128:W]
    scatter(1)
    for c in range(1, CHUNKS):
        when_slow(lambda c=c: exchange(1, c, 1).start())

    def early(c, to):
        return pltpu.make_async_remote_copy(
            src_ref=x.at[0:128, unit(c)],
            dst_ref=xp.at[:, unit(c)],
            send_sem=fwd_send.at[c],
            recv_sem=fwd_recv.at[c],
            device_id=(to, r),
            device_id_type=MESH,
        )

    def relay(c):
        return pltpu.make_async_remote_copy(
            src_ref=xp.at[:, unit(c)],
            dst_ref=xp.at[:, unit(c)],
            send_sem=relay_send.at[c],
            recv_sem=fwd_recv.at[c],
            device_id=(TARGET, r),
            device_id_type=MESH,
        )

    sends_on = jnp.logical_and(has_upper, jnp.logical_not(is_source))

    @pl.when(is_source)
    def _():
        for c in range(RELAYED):
            early(c, 0).start()

    @pl.when(sends_on)
    def _():
        for c in range(FIRST):
            early(c, upper).start()

    scatter(0)
    add_up(1)
    swap(1).start()
    add_up(0)
    gather(0)

    def far_step(c, carry):
        @pl.when(has_slow)
        def _():
            exchange(1, c, 1).wait_recv()
            blend(y, si, far_row, c)

        high, low = split(y[pl.ds(far_row, SHARED), lanes(c)])
        base = xh[:, lanes(c)]
        proj[128:W, :] += dot_rows(high, base) + (dot_rows(high, xl[:, lanes(c)]) + dot_rows(low, base))
        return carry

    lax.fori_loop(0, CHUNKS // 2, far_step, 0)
    arrived(1, 0).wait_recv()
    a_ref[64:W, 0:128] = full_g[64:W, :]
    a_ref[0:64, 0:128] = jnp.concatenate([full_g[0:64, 0:64], full_g[64:128, 0:64].T], 1)
    corner = jnp.concatenate([full_g[128:W, :].T, full_g[0:64, 64:128]], 0)
    a_ref[:, 128:LANES] = jnp.concatenate([corner, jnp.zeros((W, 64), F32)], 1)
    lax.fori_loop(CHUNKS // 2, CHUNKS, far_step, 0)
    pack_s[0:64, :] = proj[128:W, 0:128]
    pack_s[64:128, 0:64] = proj[128:W, 128:W]
    scatter(2)

    @pl.when(is_source)
    def _():
        for c in range(RELAYED, EARLY):
            early(c, upper).start()

    @pl.when(sends_on)
    def _():
        for c in range(FIRST, EARLY):
            early(c, upper).start()

    @pl.when(s == 0)
    def _():
        for c in range(RELAYED):
            early(c, upper).wait_recv()
            relay(c).start()

    def sweep_step(step, carry):
        sweep_panel(step, a_ref, p_ref, d_ref)
        return carry

    lax.fori_loop(0, 2, sweep_step, 0)
    swap(1).wait()
    mine_f[...] += other_f[...]
    gather(1)
    add_up(2)
    gather(2)
    lax.fori_loop(2, W // PANEL, sweep_step, 0)

    arrived(1, 1).wait_recv()
    pt_ref[pl.ds(rest_row, 128), 0:128] = full_f[0:128, :]
    pt_ref[pl.ds(rest_row, 64), 128:W] = full_f[128:W, 0:64]
    pt_ref[pl.ds(rest_row + 64, 64), 128:W] = full_f[128:W, 64:128]
    arrived(1, 2).wait_recv()
    pt_ref[pl.ds(far_row, 64), 0:128] = full_s[0:64, :]
    pt_ref[pl.ds(far_row, 64), 128:W] = full_s[64:128, 0:64]
    coeff = dot(pt_ref[...], -a_ref[:, 0:W])
    passed = dot(select[KEEP_DEV:W, :], coeff)
    kn[...] = passed

    late = pltpu.make_async_remote_copy(
        src_ref=kn,
        dst_ref=kp,
        send_sem=fwd_send.at[UNITS],
        recv_sem=fwd_recv.at[UNITS],
        device_id=(upper, r),
        device_id_type=MESH,
    )

    def product(c):
        place = unit(c - EARLY)
        return pltpu.make_async_remote_copy(
            src_ref=z_out.at[:, place],
            dst_ref=z_in.at[:, place],
            send_sem=fwd_send.at[c],
            recv_sem=fwd_recv.at[c],
            device_id=(upper, r),
            device_id_type=MESH,
        )

    @pl.when(has_upper)
    def _():
        late.start()
        factor = split(passed)

        def product_step(c, carry):
            z_out[:, unit(c - EARLY)] = dot_split(factor, (xh[:, unit(c)], xl[:, unit(c)]))
            product(c).start()
            return carry

        lax.fori_loop(EARLY, UNITS, product_step, 0)

    high, low = split(coeff)
    lhs_h[0:W, :] = high
    lhs_l[0:W, :] = low
    high, low = split(dot(select[0:KEEP_DEV, :], coeff))
    lhs_h[W : W + KEEP_DEV, :] = high
    lhs_l[W : W + KEEP_DEV, :] = low

    def rotate_step(c, carry):
        both = dot_split((lhs_h[...], lhs_l[...]), (xh[:, lanes(c)], xl[:, lanes(c)]))
        res_ref[:, lanes(c)] = y[:, lanes(c)] - both[0:W]
        kept_ref[:, lanes(c)] = both[W : W + KEEP_DEV]
        return carry

    lax.fori_loop(0, CHUNKS, rotate_step, 0)

    @pl.when(has_lower)
    def _():
        late.wait_recv()
        first = split(kp[:, 0:128])
        last = split(kp[:, 128:W])

        def early_step(c, carry):
            early(c, upper).wait_recv()
            extra = dot_split(first, split(xp[:, unit(c)]))
            extra = extra + dot_split(last, (xh[0:SHARED, unit(c)], xl[0:SHARED, unit(c)]))
            kept_ref[:, unit(c)] += extra
            return carry

        lax.fori_loop(0, EARLY, early_step, 0)

        def late_step(c, carry):
            product(c).wait_recv()
            kept_ref[:, unit(c)] += z_in[:, unit(c - EARLY)]
            return carry

        lax.fori_loop(EARLY, UNITS, late_step, 0)

    for kind in range(2):
        for c in range(CHUNKS):
            exchange(kind, c, 0).wait_send()
            when_slow(lambda kind=kind, c=c: exchange(kind, c, 1).wait_send())
    for phase in range(2):
        for which in range(3):
            arrived(phase, which).wait_send()

    @pl.when(s == 0)
    def _():
        for c in range(RELAYED):
            relay(c).wait_send()

    @pl.when(has_upper)
    def _():
        late.wait_send()
        for c in range(EARLY):
            early(c, upper).wait_send()
        for c in range(EARLY, UNITS):
            product(c).wait_send()


def fused_call(vectors, images, flags):
    shape = jax.ShapeDtypeStruct
    dma = pltpu.SemaphoreType.DMA

    def vmem(*dims, dtype=F32):
        return pltpu.VMEM(dims, dtype)

    big, shared = vmem(W, ROWS), vmem(SHARED, ROWS)
    half = vmem(W, ROWS, dtype=BF16)
    late_rows = vmem(KEEP_DEV, ROWS - EARLY_ROWS)
    chunks = [size // DEPTH for size in PACK]
    return pl.pallas_call(
        fused_kernel,
        out_shape=(shape((W, ROWS), F32), shape((KEEP_DEV, ROWS), F32)),
        in_specs=[HBM, HBM, VMEM],
        out_specs=(VMEM, VMEM),
        scratch_shapes=[
            big, big, half, half, shared, shared, shared, shared,
            vmem(2 * SHARED, EARLY_ROWS), late_rows, late_rows,
            vmem(W, W), vmem(W, W), vmem(W, W),
            *[vmem(size, 128) for size in PACK],
            *[vmem(count - 1, chunk, 128) for count, chunk in zip((DEPTH, DEPTH, PEERS), chunks)],
            *[vmem(chunk, 128) for chunk in chunks],
            *[vmem(size, 128) for size in PACK],
            vmem(PACK[0], 128), vmem(chunks[1], 128),
            vmem(W, LANES), vmem(PANEL, LANES), vmem(8, 8, 128), vmem(W, W), vmem(W, W), vmem(KEEP_DEV, W), vmem(KEEP_DEV, W),
            vmem(W + KEEP_DEV, W, dtype=BF16), vmem(W + KEEP_DEV, W, dtype=BF16),
            dma((2,)), dma((2, 2, CHUNKS)), dma((2, 2, CHUNKS)), dma((3, 3)), dma((3, 3)),
            dma((UNITS + 1,)), dma((UNITS + 1,)), dma((RELAYED,)),
        ],
        compiler_params=pltpu.CompilerParams(
            collective_id=0, has_side_effects=True, vmem_limit_bytes=VMEM_LIMIT
        ),
        name="fused",
    )(vectors, images, flags)


def on_device(vectors, images, kept_flags):
    residual, kept = fused_call(vectors[0].T, images[0].T, kept_flags)
    return residual.T[None], kept.T[None]


def solution(mesh):
    placed = (P("cuts", "row", None), P("cuts", "row", None), P())
    return jax.shard_map(
        on_device,
        mesh=mesh,
        in_specs=placed,
        out_specs=(P("cuts", "row", None), P("cuts", "row", None)),
        check_vma=False,
    )
```

```python
import functools

import jax
import jax.numpy as jnp
from jax import lax
from jax.experimental import pallas as pl
from jax.experimental.pallas import tpu as pltpu
from jax.sharding import PartitionSpec as P

W = 192
SHARED = 64
KEEP_DEV = 96
SLICES = 16
ROWS = 4096
PEERS = 16
DEPTH = 8
CHUNKS = 4
CHUNK = ROWS // CHUNKS
UNITS = 8
UNIT = ROWS // UNITS
FIRST = 3
EARLY = 6
RELAYED = 4
SOURCE = SLICES // 2 - 1
TARGET = SLICES // 2
EARLY_ROWS = (EARLY + 1) * UNIT
LANES = 256
PANEL = 48
VMEM_LIMIT = 48 << 20
PACK = (192, 192, 128)
F32 = jnp.float32
BF16 = jnp.bfloat16
HIGH = lax.Precision.HIGHEST
MESH = pl.DeviceIdType.MESH
HBM = pl.BlockSpec(memory_space=pltpu.HBM)
VMEM = pl.BlockSpec(memory_space=pltpu.VMEM)


def split(a):
    high = a.astype(BF16)
    return high, (a - high.astype(F32)).astype(BF16)


def dot_rows(a, b):
    return lax.dot_general(a, b, (((1,), (1,)), ((), ())), preferred_element_type=F32)


def dot_split(a, b):
    def one(x, y):
        return lax.dot_general(x, y, (((1,), (0,)), ((), ())), preferred_element_type=F32)

    return one(a[0], b[0]) + (one(a[0], b[1]) + one(a[1], b[0]))


def dot(a, b):
    return lax.dot_general(a, b, (((1,), (0,)), ((), ())), precision=HIGH, preferred_element_type=F32)


def sweep_block(kb, q, p_ref, d_ref):
    base = kb * 8
    first = 8 * q
    lane = lax.broadcasted_iota(jnp.int32, (8, LANES), 1) - base
    in_block = jnp.logical_and(lane >= 0, lane < 8)
    half = pl.ds(pl.multiple_of((kb // 16) * 128, 128), 128)
    turn = lax.rem(128 - lax.rem(base, 128), 128)
    pivots = {z: pltpu.roll(p_ref[8 * z : 8 * z + 8, half], turn, 1) for z in range(PANEL // 8)}
    for j in range(8):
        d_ref[j] = jnp.broadcast_to(pivots[q][:, j : j + 1], (8, 128))
    d = {}
    for i in range(8):
        for j in range(i, 8):
            d[i, j] = jnp.broadcast_to(d_ref[j, i : i + 1, :], (8, 128))

    def at(i, j):
        return d[min(i, j), max(i, j)]

    for k in range(8):
        pivot = 1.0 / d[k, k]
        scaled = {i: at(i, k) * pivot for i in range(8) if i != k}
        for i in range(8):
            for j in range(i, 8):
                if i != k and j != k:
                    d[i, j] = d[i, j] - scaled[i] * at(j, k)
        for i in range(8):
            if i != k:
                d[min(i, k), max(i, k)] = scaled[i]
        d[k, k] = -pivot
    rows = []
    for j in range(8):
        row = jnp.broadcast_to(p_ref[first + j : first + j + 1, :], (8, LANES))
        rows.append(jnp.where(in_block, jnp.where(lane == j, 1.0, 0.0), -row))
    solved = []
    for i in range(8):
        total = None
        for j in range(8):
            term = jnp.concatenate([at(i, j)] * 2, 1) * rows[j]
            total = term if total is None else total + term
        solved.append(total)
    for z in range(PANEL // 8):
        if z != q:
            total = jnp.where(in_block, 0.0, p_ref[8 * z : 8 * z + 8, :])
            for j in range(8):
                total = total - jnp.broadcast_to(pivots[z][:, j : j + 1], (8, LANES)) * solved[j]
            p_ref[8 * z : 8 * z + 8, :] = total
    sublane = lax.broadcasted_iota(jnp.int32, (8, LANES), 0)
    mine = solved[0]
    for i in range(1, 8):
        mine = jnp.where(sublane == i, solved[i], mine)
    p_ref[first : first + 8, :] = mine


def sweep_panel(step, a_ref, p_ref, d_ref):
    base = pl.multiple_of(step * PANEL, PANEL)
    panel = a_ref[pl.ds(base, PANEL), :]
    p_ref[...] = panel
    for q in range(PANEL // 8):
        sweep_block(step * (PANEL // 8) + q, q, p_ref, d_ref)
    swept = p_ref[...]
    update = lax.dot_general(
        panel[:, 0:W], swept, (((0,), (0,)), ((), ())), precision=HIGH, preferred_element_type=F32
    )
    lane = lax.broadcasted_iota(jnp.int32, (W, LANES), 1) - base
    a_ref[...] = jnp.where(jnp.logical_and(lane >= 0, lane < PANEL), 0.0, a_ref[...]) - update
    a_ref[pl.ds(base, PANEL), :] = swept


def fused_kernel(
    v_hbm, i_hbm, flags_hbm,
    res_ref, kept_ref,
    x, y, xh, xl, fv, fi, sv, si, xp, z_out, z_in, g_hh, g_hl, proj,
    pack_g, pack_f, pack_s, parts_g, parts_f, parts_s, mine_g, mine_f, mine_s, full_g, full_f, full_s,
    other_g, other_f,
    a_ref, p_ref, d_ref, pt_ref, select, kn, kp, lhs_h, lhs_l,
    flags_ref, load_sem, ex_send, ex_recv, sum_send, sum_recv, fwd_send, fwd_recv, relay_send,
):
    s = lax.axis_index("cuts")
    r = lax.axis_index("row")
    odd = lax.rem(s, 2)
    has_lower = s > 0
    has_upper = s < SLICES - 1
    has_slow = jnp.logical_and(has_lower, has_upper)
    upper = lax.rem(s + 1, SLICES)
    near = s + 1 - 2 * odd
    far = lax.rem(s + SLICES - 1 + 2 * odd, SLICES)
    near_row = pl.multiple_of(128 - 128 * odd, 64)
    far_row = pl.multiple_of(128 * odd, 64)
    rest_row = pl.multiple_of(64 - 64 * odd, 64)

    load_x = pltpu.make_async_copy(v_hbm, x, load_sem.at[0])
    load_y = pltpu.make_async_copy(i_hbm, y, load_sem.at[1])
    load_flags = pltpu.make_async_copy(flags_hbm, flags_ref, load_sem.at[2])
    load_flags.start()
    load_x.start()
    load_y.start()

    barrier = pltpu.get_barrier_semaphore()
    for q in (near, far):
        pl.semaphore_signal(barrier, inc=1, device_id=(q, r), device_id_type=MESH)

    def greet(i, carry):
        pl.semaphore_signal(barrier, inc=1, device_id=(s, lax.rem(r + i, PEERS)), device_id_type=MESH)
        return carry

    lax.fori_loop(1, PEERS, greet, 0)

    is_source = s == SOURCE
    at_ends = jnp.logical_or(is_source, s == TARGET)

    @pl.when(s == 0)
    def _():
        for q in (SOURCE, TARGET):
            pl.semaphore_signal(barrier, inc=1, device_id=(q, r), device_id_type=MESH)

    @pl.when(at_ends)
    def _():
        pl.semaphore_signal(barrier, inc=1, device_id=(0, r), device_id_type=MESH)


    pl.semaphore_wait(barrier, PEERS + 1 + jnp.where(s == 0, 2, jnp.where(at_ends, 1, 0)))

    def lanes(c):
        return pl.ds(pl.multiple_of(c * CHUNK, CHUNK), CHUNK)

    def unit(c):
        return pl.ds(pl.multiple_of(c * UNIT, UNIT), UNIT)

    def exchange(kind, c, way):
        return pltpu.make_async_remote_copy(
            src_ref=(v_hbm, i_hbm)[kind].at[pl.ds((near_row, far_row)[way], SHARED), lanes(c)],
            dst_ref=((fv, sv), (fi, si))[kind][way].at[:, lanes(c)],
            send_sem=ex_send.at[kind, way, c],
            recv_sem=ex_recv.at[kind, way, c],
            device_id=((near, far)[way], r),
            device_id_type=MESH,
        )

    def when_slow(action):
        pl.when(has_slow)(action)

    def blend(own, other, row, c):
        mine = own[pl.ds(row, SHARED), lanes(c)]
        own[pl.ds(row, SHARED), lanes(c)] = 0.5 * (mine + other[:, lanes(c)])

    for c in range(CHUNKS):
        when_slow(lambda c=c: exchange(0, c, 1).start())
        exchange(0, c, 0).start()
    for c in range(CHUNKS):
        exchange(1, c, 0).start()
    when_slow(lambda: exchange(1, 0, 1).start())

    load_flags.wait()
    flags = flags_ref[...].astype(F32)
    row_id = lax.broadcasted_iota(jnp.int32, (SLICES, W), 0)
    before = jnp.sum(jnp.where(row_id < s, flags, 0.0), keepdims=True)
    own_flags = jnp.sum(jnp.where(row_id == s, flags, 0.0), axis=0, keepdims=True)
    earlier = lax.broadcasted_iota(jnp.int32, (W, W), 0) < lax.broadcasted_iota(jnp.int32, (W, W), 1)
    ranks = dot(jnp.broadcast_to(own_flags, (8, W)), jnp.where(earlier, 1.0, 0.0))[0:1]
    slot = ranks + before - (s * KEEP_DEV).astype(F32)
    slot_id = lax.broadcasted_iota(jnp.int32, (W, W), 0).astype(F32)
    select[...] = jnp.where(jnp.logical_and(slot_id == slot, own_flags > 0.5), 1.0, 0.0)
    for ref in (g_hh, g_hl, proj, pack_s):
        ref[...] = jnp.zeros_like(ref)

    load_x.wait()
    load_y.wait()

    def gram_step(c, carry):
        exchange(0, c, 0).wait_recv()
        blend(x, fv, near_row, c)

        @pl.when(has_slow)
        def _():
            exchange(0, c, 1).wait_recv()
            blend(x, sv, far_row, c)

        high, low = split(x[:, lanes(c)])
        xh[:, lanes(c)] = high
        xl[:, lanes(c)] = low
        g_hh[...] += dot_rows(high, high)
        g_hl[...] += dot_rows(high, low)

        exchange(1, c, 0).wait_recv()
        blend(y, fi, near_row, c)
        rest_high, rest_low = split(y[pl.ds(rest_row, 128), lanes(c)])
        proj[0:128, :] += dot_rows(rest_high, high) + (dot_rows(rest_high, low) + dot_rows(rest_low, high))
        return carry

    lax.fori_loop(0, CHUNKS, gram_step, 0)
    sums = (
        (pack_g, parts_g, mine_g, full_g, other_g, PACK[0] // DEPTH),
        (pack_f, parts_f, mine_f, full_f, other_f, PACK[1] // DEPTH),
        (pack_s, parts_s, mine_s, full_s, None, PACK[2] // DEPTH),
    )
    partner = r + 1 - 2 * lax.rem(r, 2)

    def along_z(i):
        return lax.rem(r + 2 * i, PEERS)

    def swap(which):
        pack, _, mine, _, other, _ = sums[which]
        return pltpu.make_async_remote_copy(
            src_ref=(pack, mine)[which],
            dst_ref=other,
            send_sem=sum_send.at[2, which],
            recv_sem=sum_recv.at[2, which],
            device_id=(s, partner),
            device_id_type=MESH,
        )

    def scatter(which):
        pack, parts, _, _, other, chunk = sums[which]
        if which == 0:
            swap(0).wait()
            pack[...] += other[...]

        def one(i, carry):
            q = along_z(i) if which < 2 else lax.rem(r + i, PEERS)
            pltpu.make_async_remote_copy(
                src_ref=pack.at[pl.ds(pl.multiple_of((q // 2) * chunk, 8), chunk), :],
                dst_ref=parts.at[i - 1],
                send_sem=sum_send.at[0, which],
                recv_sem=sum_recv.at[0, which],
                device_id=(s, q),
                device_id_type=MESH,
            ).start()
            return carry

        lax.fori_loop(1, DEPTH if which < 2 else PEERS, one, 0)

    def arrived(phase, which):
        parts = sums[which][1]
        if phase == 1:
            parts = parts.at[0 : DEPTH - 1]
        return pltpu.make_async_remote_copy(
            src_ref=parts,
            dst_ref=parts,
            send_sem=sum_send.at[phase, which],
            recv_sem=sum_recv.at[phase, which],
            device_id=(s, along_z(1)),
            device_id_type=MESH,
        )

    def add_up(which):
        pack, parts, mine, _, _, chunk = sums[which]
        arrived(0, which).wait_recv()
        total = pack[pl.ds(pl.multiple_of((r // 2) * chunk, 8), chunk), :]
        for i in range(DEPTH - 1 if which < 2 else PEERS - 1):
            total = total + parts[i]
        mine[...] = total

    def gather(which):
        _, _, mine, full, _, chunk = sums[which]
        place = pl.ds(pl.multiple_of((r // 2) * chunk, 8), chunk)
        full[place, :] = mine[...]

        def one(i, carry):
            pltpu.make_async_remote_copy(
                src_ref=mine,
                dst_ref=full.at[place, :],
                send_sem=sum_send.at[1, which],
                recv_sem=sum_recv.at[1, which],
                device_id=(s, along_z(i)),
                device_id_type=MESH,
            ).start()
            return carry

        lax.fori_loop(1, DEPTH, one, 0)

    gram = g_hh[...] + (g_hl[...] + g_hl[...].T)
    pack_g[:, 0:64] = gram[:, 0:64]
    pack_g[64:W, 64:128] = gram[64:W, 64:128]
    pack_g[0:64, 64:128] = gram[128:W, 128:W]
    swap(0).start()
    pack_f[0:128, :] = proj[0:128, 0:128]
    pack_f[128:W, 0:64] = proj[0:64, 128:W]
    pack_f[128:W, 64:128] = proj[64:128, 128:W]
    scatter(1)
    for c in range(1, CHUNKS):
        when_slow(lambda c=c: exchange(1, c, 1).start())

    def early(c, to):
        return pltpu.make_async_remote_copy(
            src_ref=x.at[0:128, unit(c)],
            dst_ref=xp.at[:, unit(c)],
            send_sem=fwd_send.at[c],
            recv_sem=fwd_recv.at[c],
            device_id=(to, r),
            device_id_type=MESH,
        )

    def relay(c):
        return pltpu.make_async_remote_copy(
            src_ref=xp.at[:, unit(c)],
            dst_ref=xp.at[:, unit(c)],
            send_sem=relay_send.at[c],
            recv_sem=fwd_recv.at[c],
            device_id=(TARGET, r),
            device_id_type=MESH,
        )

    sends_on = jnp.logical_and(has_upper, jnp.logical_not(is_source))
    sent_early = EARLY + jnp.where(is_source, 1, 0)
    got_early = EARLY + jnp.where(s == TARGET, 1, 0)

    @pl.when(is_source)
    def _():
        for c in range(RELAYED):
            early(c, 0).start()

    @pl.when(sends_on)
    def _():
        for c in range(FIRST):
            early(c, upper).start()

    scatter(0)
    add_up(1)
    swap(1).start()
    add_up(0)
    gather(0)

    def far_step(c, carry):
        @pl.when(has_slow)
        def _():
            exchange(1, c, 1).wait_recv()
            blend(y, si, far_row, c)

        high, low = split(y[pl.ds(far_row, SHARED), lanes(c)])
        base = xh[:, lanes(c)]
        proj[128:W, :] += dot_rows(high, base) + (dot_rows(high, xl[:, lanes(c)]) + dot_rows(low, base))
        return carry

    lax.fori_loop(0, CHUNKS, far_step, 0)
    pack_s[0:64, :] = proj[128:W, 0:128]
    pack_s[64:128, 0:64] = proj[128:W, 128:W]
    scatter(2)

    @pl.when(is_source)
    def _():
        for c in range(RELAYED, EARLY + 1):
            early(c, upper).start()

    @pl.when(sends_on)
    def _():
        for c in range(FIRST, EARLY):
            early(c, upper).start()

    @pl.when(s == 0)
    def _():
        for c in range(RELAYED):
            early(c, upper).wait_recv()
            relay(c).start()

    arrived(1, 0).wait_recv()
    a_ref[64:W, 0:128] = full_g[64:W, :]
    a_ref[0:64, 0:128] = jnp.concatenate([full_g[0:64, 0:64], full_g[64:128, 0:64].T], 1)
    corner = jnp.concatenate([full_g[128:W, :].T, full_g[0:64, 64:128]], 0)
    a_ref[:, 128:LANES] = jnp.concatenate([corner, jnp.zeros((W, 64), F32)], 1)

    def sweep_step(step, carry):
        sweep_panel(step, a_ref, p_ref, d_ref)
        return carry

    lax.fori_loop(0, 2, sweep_step, 0)
    swap(1).wait()
    mine_f[...] += other_f[...]
    gather(1)
    add_up(2)
    gather(2)
    lax.fori_loop(2, W // PANEL, sweep_step, 0)

    arrived(1, 1).wait_recv()
    pt_ref[pl.ds(rest_row, 128), 0:128] = full_f[0:128, :]
    pt_ref[pl.ds(rest_row, 64), 128:W] = full_f[128:W, 0:64]
    pt_ref[pl.ds(rest_row + 64, 64), 128:W] = full_f[128:W, 64:128]
    arrived(1, 2).wait_recv()
    pt_ref[pl.ds(far_row, 64), 0:128] = full_s[0:64, :]
    pt_ref[pl.ds(far_row, 64), 128:W] = full_s[64:128, 0:64]
    coeff = dot(pt_ref[...], -a_ref[:, 0:W])
    passed = dot(select[KEEP_DEV:W, :], coeff)
    kn[...] = passed

    late = pltpu.make_async_remote_copy(
        src_ref=kn,
        dst_ref=kp,
        send_sem=fwd_send.at[UNITS],
        recv_sem=fwd_recv.at[UNITS],
        device_id=(upper, r),
        device_id_type=MESH,
    )

    def product(c):
        place = unit(c - EARLY)
        return pltpu.make_async_remote_copy(
            src_ref=z_out.at[:, place],
            dst_ref=z_in.at[:, place],
            send_sem=fwd_send.at[c],
            recv_sem=fwd_recv.at[c],
            device_id=(upper, r),
            device_id_type=MESH,
        )

    @pl.when(has_upper)
    def _():
        late.start()
        factor = split(passed)

        def product_step(c, carry):
            z_out[:, unit(c - EARLY)] = dot_split(factor, (xh[:, unit(c)], xl[:, unit(c)]))
            product(c).start()
            return carry

        lax.fori_loop(sent_early, UNITS, product_step, 0)

    high, low = split(coeff)
    lhs_h[0:W, :] = high
    lhs_l[0:W, :] = low
    high, low = split(dot(select[0:KEEP_DEV, :], coeff))
    lhs_h[W : W + KEEP_DEV, :] = high
    lhs_l[W : W + KEEP_DEV, :] = low

    def rotate_step(c, carry):
        both = dot_split((lhs_h[...], lhs_l[...]), (xh[:, lanes(c)], xl[:, lanes(c)]))
        res_ref[:, lanes(c)] = y[:, lanes(c)] - both[0:W]
        kept_ref[:, lanes(c)] = both[W : W + KEEP_DEV]
        return carry

    lax.fori_loop(0, CHUNKS, rotate_step, 0)

    @pl.when(has_lower)
    def _():
        late.wait_recv()
        first = split(kp[:, 0:128])
        last = split(kp[:, 128:W])

        def early_step(c, carry):
            early(c, upper).wait_recv()
            extra = dot_split(first, split(xp[:, unit(c)]))
            extra = extra + dot_split(last, (xh[0:SHARED, unit(c)], xl[0:SHARED, unit(c)]))
            kept_ref[:, unit(c)] += extra
            return carry

        lax.fori_loop(0, got_early, early_step, 0)

        def late_step(c, carry):
            product(c).wait_recv()
            kept_ref[:, unit(c)] += z_in[:, unit(c - EARLY)]
            return carry

        lax.fori_loop(got_early, UNITS, late_step, 0)

    for kind in range(2):
        for c in range(CHUNKS):
            exchange(kind, c, 0).wait_send()
            when_slow(lambda kind=kind, c=c: exchange(kind, c, 1).wait_send())
    for phase in range(2):
        for which in range(3):
            arrived(phase, which).wait_send()

    @pl.when(s == 0)
    def _():
        for c in range(RELAYED):
            relay(c).wait_send()

    @pl.when(has_upper)
    def _():
        late.wait_send()
        for c in range(EARLY):
            early(c, upper).wait_send()
        for c in range(EARLY + 1, UNITS):
            product(c).wait_send()

    @pl.when(is_source)
    def _():
        early(EARLY, upper).wait_send()

    @pl.when(sends_on)
    def _():
        product(EARLY).wait_send()


def fused_call(vectors, images, flags):
    shape = jax.ShapeDtypeStruct
    dma = pltpu.SemaphoreType.DMA

    def vmem(*dims, dtype=F32):
        return pltpu.VMEM(dims, dtype)

    big, shared = vmem(W, ROWS), vmem(SHARED, ROWS)
    half = vmem(W, ROWS, dtype=BF16)
    late_rows = vmem(KEEP_DEV, (UNITS - EARLY) * UNIT)
    chunks = [size // DEPTH for size in PACK]
    return pl.pallas_call(
        fused_kernel,
        out_shape=(shape((W, ROWS), F32), shape((KEEP_DEV, ROWS), F32)),
        in_specs=[HBM, HBM, HBM],
        out_specs=(VMEM, VMEM),
        scratch_shapes=[
            big, big, half, half, shared, shared, shared, shared,
            vmem(2 * SHARED, EARLY_ROWS), late_rows, late_rows,
            vmem(W, W), vmem(W, W), vmem(W, W),
            *[vmem(size, 128) for size in PACK],
            *[vmem(count - 1, chunk, 128) for count, chunk in zip((DEPTH, DEPTH, PEERS), chunks)],
            *[vmem(chunk, 128) for chunk in chunks],
            *[vmem(size, 128) for size in PACK],
            vmem(PACK[0], 128), vmem(chunks[1], 128),
            vmem(W, LANES), vmem(PANEL, LANES), vmem(8, 8, 128), vmem(W, W), vmem(W, W), vmem(KEEP_DEV, W), vmem(KEEP_DEV, W),
            vmem(W + KEEP_DEV, W, dtype=BF16), vmem(W + KEEP_DEV, W, dtype=BF16),
            vmem(SLICES, W, dtype=jnp.int32), dma((3,)), dma((2, 2, CHUNKS)), dma((2, 2, CHUNKS)), dma((3, 3)), dma((3, 3)),
            dma((UNITS + 1,)), dma((UNITS + 1,)), dma((RELAYED,)),
        ],
        compiler_params=pltpu.CompilerParams(
            collective_id=0, has_side_effects=True, vmem_limit_bytes=VMEM_LIMIT
        ),
        name="fused",
    )(vectors, images, flags)


def on_device(vectors, images, kept_flags):
    kept_flags = pltpu.with_memory_space_constraint(kept_flags, pltpu.HBM)
    residual, kept = fused_call(vectors[0].T, images[0].T, kept_flags)
    return residual.T[None], kept.T[None]


def solution(mesh):
    placed = (P("cuts", "row", None), P("cuts", "row", None), P())
    return jax.shard_map(
        on_device,
        mesh=mesh,
        in_specs=placed,
        out_specs=(P("cuts", "row", None), P("cuts", "row", None)),
        check_vma=False,
    )
```

```python
import functools

import jax
import jax.numpy as jnp
from jax import lax
from jax.experimental import pallas as pl
from jax.experimental.pallas import tpu as pltpu
from jax.sharding import PartitionSpec as P

W = 192
SHARED = 64
KEEP_DEV = 96
SLICES = 16
ROWS = 4096
PEERS = 16
DEPTH = 8
CHUNKS = 4
CHUNK = ROWS // CHUNKS
UNITS = 8
UNIT = ROWS // UNITS
FIRST = 4
EARLY = 6
RELAYED = 4
SOURCE = SLICES // 2 - 1
TARGET = SLICES // 2
EARLY_ROWS = (EARLY + 1) * UNIT
LANES = 256
PANEL = 48
VMEM_LIMIT = 48 << 20
PACK = (192, 192, 128)
F32 = jnp.float32
BF16 = jnp.bfloat16
HIGH = lax.Precision.HIGHEST
MESH = pl.DeviceIdType.MESH
HBM = pl.BlockSpec(memory_space=pltpu.HBM)
VMEM = pl.BlockSpec(memory_space=pltpu.VMEM)


def split(a):
    high = a.astype(BF16)
    return high, (a - high.astype(F32)).astype(BF16)


def dot_rows(a, b):
    return lax.dot_general(a, b, (((1,), (1,)), ((), ())), preferred_element_type=F32)


def dot_split(a, b):
    def one(x, y):
        return lax.dot_general(x, y, (((1,), (0,)), ((), ())), preferred_element_type=F32)

    return one(a[0], b[0]) + (one(a[0], b[1]) + one(a[1], b[0]))


def dot(a, b):
    return lax.dot_general(a, b, (((1,), (0,)), ((), ())), precision=HIGH, preferred_element_type=F32)


def sweep_block(kb, q, p_ref, d_ref):
    base = kb * 8
    first = 8 * q
    lane = lax.broadcasted_iota(jnp.int32, (8, LANES), 1) - base
    in_block = jnp.logical_and(lane >= 0, lane < 8)
    half = pl.ds(pl.multiple_of((kb // 16) * 128, 128), 128)
    turn = lax.rem(128 - lax.rem(base, 128), 128)
    pivots = {z: pltpu.roll(p_ref[8 * z : 8 * z + 8, half], turn, 1) for z in range(PANEL // 8)}
    for j in range(8):
        d_ref[j] = jnp.broadcast_to(pivots[q][:, j : j + 1], (8, 128))
    d = {}
    for i in range(8):
        for j in range(i, 8):
            d[i, j] = jnp.broadcast_to(d_ref[j, i : i + 1, :], (8, 128))

    def at(i, j):
        return d[min(i, j), max(i, j)]

    for k in range(8):
        pivot = 1.0 / d[k, k]
        scaled = {i: at(i, k) * pivot for i in range(8) if i != k}
        for i in range(8):
            for j in range(i, 8):
                if i != k and j != k:
                    d[i, j] = d[i, j] - scaled[i] * at(j, k)
        for i in range(8):
            if i != k:
                d[min(i, k), max(i, k)] = scaled[i]
        d[k, k] = -pivot
    rows = []
    for j in range(8):
        row = jnp.broadcast_to(p_ref[first + j : first + j + 1, :], (8, LANES))
        rows.append(jnp.where(in_block, jnp.where(lane == j, 1.0, 0.0), -row))
    solved = []
    for i in range(8):
        total = None
        for j in range(8):
            term = jnp.concatenate([at(i, j)] * 2, 1) * rows[j]
            total = term if total is None else total + term
        solved.append(total)
    for z in range(PANEL // 8):
        if z != q:
            total = jnp.where(in_block, 0.0, p_ref[8 * z : 8 * z + 8, :])
            for j in range(8):
                total = total - jnp.broadcast_to(pivots[z][:, j : j + 1], (8, LANES)) * solved[j]
            p_ref[8 * z : 8 * z + 8, :] = total
    sublane = lax.broadcasted_iota(jnp.int32, (8, LANES), 0)
    mine = solved[0]
    for i in range(1, 8):
        mine = jnp.where(sublane == i, solved[i], mine)
    p_ref[first : first + 8, :] = mine


def sweep_panel(step, a_ref, p_ref, d_ref):
    base = pl.multiple_of(step * PANEL, PANEL)
    panel = a_ref[pl.ds(base, PANEL), :]
    p_ref[...] = panel
    for q in range(PANEL // 8):
        sweep_block(step * (PANEL // 8) + q, q, p_ref, d_ref)
    swept = p_ref[...]
    update = lax.dot_general(
        panel[:, 0:W], swept, (((0,), (0,)), ((), ())), precision=HIGH, preferred_element_type=F32
    )
    lane = lax.broadcasted_iota(jnp.int32, (W, LANES), 1) - base
    a_ref[...] = jnp.where(jnp.logical_and(lane >= 0, lane < PANEL), 0.0, a_ref[...]) - update
    a_ref[pl.ds(base, PANEL), :] = swept


def fused_kernel(
    v_hbm, i_hbm, flags_hbm,
    res_ref, kept_ref,
    x, y, xh, xl, fv, fi, sv, si, xp, z_out, z_in, g_hh, g_hl, proj,
    pack_g, pack_f, pack_s, parts_g, parts_f, parts_s, mine_g, mine_f, mine_s, full_g, full_f, full_s,
    other_g, other_f,
    a_ref, p_ref, d_ref, pt_ref, select, kn, kp, lhs_h, lhs_l,
    flags_ref, load_sem, ex_send, ex_recv, sum_send, sum_recv, fwd_send, fwd_recv, relay_send,
):
    s = lax.axis_index("cuts")
    r = lax.axis_index("row")
    odd = lax.rem(s, 2)
    has_lower = s > 0
    has_upper = s < SLICES - 1
    has_slow = jnp.logical_and(has_lower, has_upper)
    upper = lax.rem(s + 1, SLICES)
    near = s + 1 - 2 * odd
    far = lax.rem(s + SLICES - 1 + 2 * odd, SLICES)
    near_row = pl.multiple_of(128 - 128 * odd, 64)
    far_row = pl.multiple_of(128 * odd, 64)
    rest_row = pl.multiple_of(64 - 64 * odd, 64)

    load_x = pltpu.make_async_copy(v_hbm, x, load_sem.at[0])
    load_y = pltpu.make_async_copy(i_hbm, y, load_sem.at[1])
    load_flags = pltpu.make_async_copy(flags_hbm, flags_ref, load_sem.at[2])
    load_flags.start()
    load_x.start()
    load_y.start()

    barrier = pltpu.get_barrier_semaphore()
    for q in (near, far):
        pl.semaphore_signal(barrier, inc=1, device_id=(q, r), device_id_type=MESH)

    def greet(i, carry):
        pl.semaphore_signal(barrier, inc=1, device_id=(s, lax.rem(r + i, PEERS)), device_id_type=MESH)
        return carry

    lax.fori_loop(1, PEERS, greet, 0)

    is_source = s == SOURCE
    at_ends = jnp.logical_or(is_source, s == TARGET)

    @pl.when(s == 0)
    def _():
        for q in (SOURCE, TARGET):
            pl.semaphore_signal(barrier, inc=1, device_id=(q, r), device_id_type=MESH)

    @pl.when(at_ends)
    def _():
        pl.semaphore_signal(barrier, inc=1, device_id=(0, r), device_id_type=MESH)


    pl.semaphore_wait(barrier, PEERS + 1 + jnp.where(s == 0, 2, jnp.where(at_ends, 1, 0)))

    def lanes(c):
        return pl.ds(pl.multiple_of(c * CHUNK, CHUNK), CHUNK)

    def unit(c):
        return pl.ds(pl.multiple_of(c * UNIT, UNIT), UNIT)

    def exchange(kind, c, way):
        return pltpu.make_async_remote_copy(
            src_ref=(v_hbm, i_hbm)[kind].at[pl.ds((near_row, far_row)[way], SHARED), lanes(c)],
            dst_ref=((fv, sv), (fi, si))[kind][way].at[:, lanes(c)],
            send_sem=ex_send.at[kind, way, c],
            recv_sem=ex_recv.at[kind, way, c],
            device_id=((near, far)[way], r),
            device_id_type=MESH,
        )

    def when_slow(action):
        pl.when(has_slow)(action)

    def blend(own, other, row, c):
        mine = own[pl.ds(row, SHARED), lanes(c)]
        own[pl.ds(row, SHARED), lanes(c)] = 0.5 * (mine + other[:, lanes(c)])

    for c in range(CHUNKS):
        when_slow(lambda c=c: exchange(0, c, 1).start())
        exchange(0, c, 0).start()
    for c in range(CHUNKS):
        exchange(1, c, 0).start()
    when_slow(lambda: exchange(1, 0, 1).start())

    load_flags.wait()
    flags = flags_ref[...].astype(F32)
    row_id = lax.broadcasted_iota(jnp.int32, (SLICES, W), 0)
    before = jnp.sum(jnp.where(row_id < s, flags, 0.0), keepdims=True)
    own_flags = jnp.sum(jnp.where(row_id == s, flags, 0.0), axis=0, keepdims=True)
    earlier = lax.broadcasted_iota(jnp.int32, (W, W), 0) < lax.broadcasted_iota(jnp.int32, (W, W), 1)
    ranks = dot(jnp.broadcast_to(own_flags, (8, W)), jnp.where(earlier, 1.0, 0.0))[0:1]
    slot = ranks + before - (s * KEEP_DEV).astype(F32)
    slot_id = lax.broadcasted_iota(jnp.int32, (W, W), 0).astype(F32)
    select[...] = jnp.where(jnp.logical_and(slot_id == slot, own_flags > 0.5), 1.0, 0.0)
    for ref in (g_hh, g_hl, proj, pack_s):
        ref[...] = jnp.zeros_like(ref)

    load_x.wait()
    load_y.wait()

    def gram_step(c, carry):
        exchange(0, c, 0).wait_recv()
        blend(x, fv, near_row, c)

        @pl.when(has_slow)
        def _():
            exchange(0, c, 1).wait_recv()
            blend(x, sv, far_row, c)

        high, low = split(x[:, lanes(c)])
        xh[:, lanes(c)] = high
        xl[:, lanes(c)] = low
        g_hh[...] += dot_rows(high, high)
        g_hl[...] += dot_rows(high, low)

        exchange(1, c, 0).wait_recv()
        blend(y, fi, near_row, c)
        rest_high, rest_low = split(y[pl.ds(rest_row, 128), lanes(c)])
        proj[0:128, :] += dot_rows(rest_high, high) + (dot_rows(rest_high, low) + dot_rows(rest_low, high))
        return carry

    lax.fori_loop(0, CHUNKS, gram_step, 0)
    sums = (
        (pack_g, parts_g, mine_g, full_g, other_g, PACK[0] // DEPTH),
        (pack_f, parts_f, mine_f, full_f, other_f, PACK[1] // DEPTH),
        (pack_s, parts_s, mine_s, full_s, None, PACK[2] // DEPTH),
    )
    partner = r + 1 - 2 * lax.rem(r, 2)

    def along_z(i):
        return lax.rem(r + 2 * i, PEERS)

    def swap(which):
        pack, _, mine, _, other, _ = sums[which]
        return pltpu.make_async_remote_copy(
            src_ref=(pack, mine)[which],
            dst_ref=other,
            send_sem=sum_send.at[2, which],
            recv_sem=sum_recv.at[2, which],
            device_id=(s, partner),
            device_id_type=MESH,
        )

    def scatter(which):
        pack, parts, _, _, other, chunk = sums[which]
        if which == 0:
            swap(0).wait()
            pack[...] += other[...]

        def one(i, carry):
            q = along_z(i) if which < 2 else lax.rem(r + i, PEERS)
            pltpu.make_async_remote_copy(
                src_ref=pack.at[pl.ds(pl.multiple_of((q // 2) * chunk, 8), chunk), :],
                dst_ref=parts.at[i - 1],
                send_sem=sum_send.at[0, which],
                recv_sem=sum_recv.at[0, which],
                device_id=(s, q),
                device_id_type=MESH,
            ).start()
            return carry

        lax.fori_loop(1, DEPTH if which < 2 else PEERS, one, 0)

    def arrived(phase, which):
        parts = sums[which][1]
        if phase == 1:
            parts = parts.at[0 : DEPTH - 1]
        return pltpu.make_async_remote_copy(
            src_ref=parts,
            dst_ref=parts,
            send_sem=sum_send.at[phase, which],
            recv_sem=sum_recv.at[phase, which],
            device_id=(s, along_z(1)),
            device_id_type=MESH,
        )

    def add_up(which):
        pack, parts, mine, _, _, chunk = sums[which]
        arrived(0, which).wait_recv()
        total = pack[pl.ds(pl.multiple_of((r // 2) * chunk, 8), chunk), :]
        for i in range(DEPTH - 1 if which < 2 else PEERS - 1):
            total = total + parts[i]
        mine[...] = total

    def gather(which):
        _, _, mine, full, _, chunk = sums[which]
        place = pl.ds(pl.multiple_of((r // 2) * chunk, 8), chunk)
        full[place, :] = mine[...]

        def one(i, carry):
            pltpu.make_async_remote_copy(
                src_ref=mine,
                dst_ref=full.at[place, :],
                send_sem=sum_send.at[1, which],
                recv_sem=sum_recv.at[1, which],
                device_id=(s, along_z(i)),
                device_id_type=MESH,
            ).start()
            return carry

        lax.fori_loop(1, DEPTH, one, 0)

    gram = g_hh[...] + (g_hl[...] + g_hl[...].T)
    pack_g[:, 0:64] = gram[:, 0:64]
    pack_g[64:W, 64:128] = gram[64:W, 64:128]
    pack_g[0:64, 64:128] = gram[128:W, 128:W]
    swap(0).start()
    pack_f[0:128, :] = proj[0:128, 0:128]
    pack_f[128:W, 0:64] = proj[0:64, 128:W]
    pack_f[128:W, 64:128] = proj[64:128, 128:W]
    scatter(1)
    for c in range(1, CHUNKS):
        when_slow(lambda c=c: exchange(1, c, 1).start())

    def early(c, to):
        return pltpu.make_async_remote_copy(
            src_ref=x.at[0:128, unit(c)],
            dst_ref=xp.at[:, unit(c)],
            send_sem=fwd_send.at[c],
            recv_sem=fwd_recv.at[c],
            device_id=(to, r),
            device_id_type=MESH,
        )

    def relay(c):
        return pltpu.make_async_remote_copy(
            src_ref=xp.at[:, unit(c)],
            dst_ref=xp.at[:, unit(c)],
            send_sem=relay_send.at[c],
            recv_sem=fwd_recv.at[c],
            device_id=(TARGET, r),
            device_id_type=MESH,
        )

    sends_on = jnp.logical_and(has_upper, jnp.logical_not(is_source))
    sent_early = EARLY + jnp.where(is_source, 1, 0)
    got_early = EARLY + jnp.where(s == TARGET, 1, 0)

    @pl.when(is_source)
    def _():
        for c in range(RELAYED):
            early(c, 0).start()

    @pl.when(sends_on)
    def _():
        for c in range(FIRST):
            early(c, upper).start()

    scatter(0)
    add_up(1)
    swap(1).start()
    add_up(0)
    gather(0)

    def far_step(c, carry):
        @pl.when(has_slow)
        def _():
            exchange(1, c, 1).wait_recv()
            blend(y, si, far_row, c)

        high, low = split(y[pl.ds(far_row, SHARED), lanes(c)])
        base = xh[:, lanes(c)]
        proj[128:W, :] += dot_rows(high, base) + (dot_rows(high, xl[:, lanes(c)]) + dot_rows(low, base))
        return carry

    lax.fori_loop(0, CHUNKS, far_step, 0)
    pack_s[0:64, :] = proj[128:W, 0:128]
    pack_s[64:128, 0:64] = proj[128:W, 128:W]
    scatter(2)

    @pl.when(is_source)
    def _():
        for c in range(RELAYED, EARLY + 1):
            early(c, upper).start()

    @pl.when(sends_on)
    def _():
        for c in range(FIRST, EARLY):
            early(c, upper).start()

    @pl.when(s == 0)
    def _():
        for c in range(RELAYED):
            early(c, upper).wait_recv()
            relay(c).start()

    arrived(1, 0).wait_recv()
    a_ref[64:W, 0:128] = full_g[64:W, :]
    a_ref[0:64, 0:128] = jnp.concatenate([full_g[0:64, 0:64], full_g[64:128, 0:64].T], 1)
    corner = jnp.concatenate([full_g[128:W, :].T, full_g[0:64, 64:128]], 0)
    a_ref[:, 128:LANES] = jnp.concatenate([corner, jnp.zeros((W, 64), F32)], 1)

    def sweep_step(step, carry):
        sweep_panel(step, a_ref, p_ref, d_ref)
        return carry

    lax.fori_loop(0, 2, sweep_step, 0)
    swap(1).wait()
    mine_f[...] += other_f[...]
    gather(1)
    add_up(2)
    gather(2)
    lax.fori_loop(2, W // PANEL, sweep_step, 0)

    arrived(1, 1).wait_recv()
    pt_ref[pl.ds(rest_row, 128), 0:128] = full_f[0:128, :]
    pt_ref[pl.ds(rest_row, 64), 128:W] = full_f[128:W, 0:64]
    pt_ref[pl.ds(rest_row + 64, 64), 128:W] = full_f[128:W, 64:128]
    arrived(1, 2).wait_recv()
    pt_ref[pl.ds(far_row, 64), 0:128] = full_s[0:64, :]
    pt_ref[pl.ds(far_row, 64), 128:W] = full_s[64:128, 0:64]
    coeff = dot(pt_ref[...], -a_ref[:, 0:W])
    passed = dot(select[KEEP_DEV:W, :], coeff)
    kn[...] = passed

    late = pltpu.make_async_remote_copy(
        src_ref=kn,
        dst_ref=kp,
        send_sem=fwd_send.at[UNITS],
        recv_sem=fwd_recv.at[UNITS],
        device_id=(upper, r),
        device_id_type=MESH,
    )

    def product(c):
        place = unit(c - EARLY)
        return pltpu.make_async_remote_copy(
            src_ref=z_out.at[:, place],
            dst_ref=z_in.at[:, place],
            send_sem=fwd_send.at[c],
            recv_sem=fwd_recv.at[c],
            device_id=(upper, r),
            device_id_type=MESH,
        )

    @pl.when(has_upper)
    def _():
        late.start()
        factor = split(passed)

        def product_step(c, carry):
            z_out[:, unit(c - EARLY)] = dot_split(factor, (xh[:, unit(c)], xl[:, unit(c)]))
            product(c).start()
            return carry

        lax.fori_loop(sent_early, UNITS, product_step, 0)

    high, low = split(coeff)
    lhs_h[0:W, :] = high
    lhs_l[0:W, :] = low
    high, low = split(dot(select[0:KEEP_DEV, :], coeff))
    lhs_h[W : W + KEEP_DEV, :] = high
    lhs_l[W : W + KEEP_DEV, :] = low

    def rotate_step(c, carry):
        both = dot_split((lhs_h[...], lhs_l[...]), (xh[:, lanes(c)], xl[:, lanes(c)]))
        res_ref[:, lanes(c)] = y[:, lanes(c)] - both[0:W]
        kept_ref[:, lanes(c)] = both[W : W + KEEP_DEV]
        return carry

    lax.fori_loop(0, CHUNKS, rotate_step, 0)

    @pl.when(has_lower)
    def _():
        late.wait_recv()
        first = split(kp[:, 0:128])
        last = split(kp[:, 128:W])

        def early_step(c, carry):
            early(c, upper).wait_recv()
            extra = dot_split(first, split(xp[:, unit(c)]))
            extra = extra + dot_split(last, (xh[0:SHARED, unit(c)], xl[0:SHARED, unit(c)]))
            kept_ref[:, unit(c)] += extra
            return carry

        lax.fori_loop(0, got_early, early_step, 0)

        def late_step(c, carry):
            product(c).wait_recv()
            kept_ref[:, unit(c)] += z_in[:, unit(c - EARLY)]
            return carry

        lax.fori_loop(got_early, UNITS, late_step, 0)

    for kind in range(2):
        for c in range(CHUNKS):
            exchange(kind, c, 0).wait_send()
            when_slow(lambda kind=kind, c=c: exchange(kind, c, 1).wait_send())
    for phase in range(2):
        for which in range(3):
            arrived(phase, which).wait_send()

    @pl.when(s == 0)
    def _():
        for c in range(RELAYED):
            relay(c).wait_send()

    @pl.when(has_upper)
    def _():
        late.wait_send()
        for c in range(EARLY):
            early(c, upper).wait_send()
        for c in range(EARLY + 1, UNITS):
            product(c).wait_send()

    @pl.when(is_source)
    def _():
        early(EARLY, upper).wait_send()

    @pl.when(sends_on)
    def _():
        product(EARLY).wait_send()


def fused_call(vectors, images, flags):
    shape = jax.ShapeDtypeStruct
    dma = pltpu.SemaphoreType.DMA

    def vmem(*dims, dtype=F32):
        return pltpu.VMEM(dims, dtype)

    big, shared = vmem(W, ROWS), vmem(SHARED, ROWS)
    half = vmem(W, ROWS, dtype=BF16)
    late_rows = vmem(KEEP_DEV, (UNITS - EARLY) * UNIT)
    chunks = [size // DEPTH for size in PACK]
    return pl.pallas_call(
        fused_kernel,
        out_shape=(shape((W, ROWS), F32), shape((KEEP_DEV, ROWS), F32)),
        in_specs=[HBM, HBM, HBM],
        out_specs=(VMEM, VMEM),
        scratch_shapes=[
            big, big, half, half, shared, shared, shared, shared,
            vmem(2 * SHARED, EARLY_ROWS), late_rows, late_rows,
            vmem(W, W), vmem(W, W), vmem(W, W),
            *[vmem(size, 128) for size in PACK],
            *[vmem(count - 1, chunk, 128) for count, chunk in zip((DEPTH, DEPTH, PEERS), chunks)],
            *[vmem(chunk, 128) for chunk in chunks],
            *[vmem(size, 128) for size in PACK],
            vmem(PACK[0], 128), vmem(chunks[1], 128),
            vmem(W, LANES), vmem(PANEL, LANES), vmem(8, 8, 128), vmem(W, W), vmem(W, W), vmem(KEEP_DEV, W), vmem(KEEP_DEV, W),
            vmem(W + KEEP_DEV, W, dtype=BF16), vmem(W + KEEP_DEV, W, dtype=BF16),
            vmem(SLICES, W, dtype=jnp.int32), dma((3,)), dma((2, 2, CHUNKS)), dma((2, 2, CHUNKS)), dma((3, 3)), dma((3, 3)),
            dma((UNITS + 1,)), dma((UNITS + 1,)), dma((RELAYED,)),
        ],
        compiler_params=pltpu.CompilerParams(
            collective_id=0, has_side_effects=True, vmem_limit_bytes=VMEM_LIMIT
        ),
        name="fused",
    )(vectors, images, flags)


def on_device(vectors, images, kept_flags):
    kept_flags = pltpu.with_memory_space_constraint(kept_flags, pltpu.HBM)
    residual, kept = fused_call(vectors[0].T, images[0].T, kept_flags)
    return residual.T[None], kept.T[None]


def solution(mesh):
    placed = (P("cuts", "row", None), P("cuts", "row", None), P())
    return jax.shard_map(
        on_device,
        mesh=mesh,
        in_specs=placed,
        out_specs=(P("cuts", "row", None), P("cuts", "row", None)),
        check_vma=False,
    )
```
